32 devices in a mesh: span: 8 (over y, x, core), depth: 4 (over z).
Axes of the slice: x: 2, y: 2, z: 4, core: 2. Of those that a mesh axis runs over, the one named last changes fastest.
Arguments:
- shell_temp: float32 [8, 1024, 256], P('span', 'depth'), may hold values from -6 to 6
- contact_gain: float32 [8, 1024, 256], P('span', 'depth'), may hold values from 0.2 to 2
- die_temp: float32 [48, 256, 1024], P(None, 'span', 'depth'), may hold values from -4 to 4
- diffusivity: float32 [48, 256, 1024], P(None, 'span', 'depth'), may hold values from 0.02 to 0.12
- routes: int32 [8, 1024, 1], P('span', 'depth'), may hold values from 0 to 7; in each aligned block of 256 rows (0 to 255, 256 to 511, ..., all dimensions but the last counted through in order) at most 64 rows name the same one
- tile_rows: int32 [8, 1024], P('span', 'depth'), may hold values from 0 to 31
- closed: int32 [8, 1024], P('span', 'depth'), may hold values 0 or 1
Outputs:
- shell_next: float32 [8, 1024, 256], P('span', 'depth')
- die_next: float32 [48, 256, 1024], P(None, 'span', 'depth')
The draws below stay inside these ranges and needn't reach their ends.
Inputs may be any that keep to these rules, and one draw needn't show every extreme that they name: `routes`: among the 256 block rows of one device, at most 64 name the same span index, and in some device's rows one span index is named exactly 64 times.
All inputs are finite; a program needn't handle non-finite values. No bound on the sum of `closed` on one device may be relied on, other than what follows from the above.
Results may differ from the reference program's by a relative error of at most 0.00025.
Values sent between devices are 32-bit elements; how exact they have to be, the bound alone decides.
A program may use at most 128 MiB of HBM per device.

```python
import math
import jax
import jax.numpy as jnp
import numpy as np

NB = 256
SB = 256
CX = 32
DZ = 48
CAP = 64
ROWS = 1024
NX = 256
NY = 1024
N_SPAN = 8
N_DEPTH = 4


def with_ends(values, key, least, top_value):
    longest = values.shape.index(max(values.shape))
    spots = []
    for shift in (0, 1):
        where = [jax.random.randint(jax.random.fold_in(key, axis), (), 0, length) for axis, length in enumerate(values.shape)]
        where[longest] = (where[longest] + shift) % values.shape[longest]
        spots.append(tuple(where))
    return values.at[spots[0]].set(least).at[spots[1]].set(top_value)


def shard_levels(own_key, dims, split, least, largest):
    def one(dim, blocks):
        draws = jax.random.uniform(jax.random.fold_in(jax.random.fold_in(own_key, 6), dim), (blocks,), jnp.float32, least / len(split), largest / len(split))
        return jnp.repeat(jnp.exp(draws), dims[dim] // blocks).reshape((-1,) + (1,) * (len(dims) - dim - 1))

    level = one(*split[0])
    for cut in split[1:]:
        level = level * one(*cut)
    return level


def shared_out(stream_key, own, number, rows, amount, top, limit, lean):
    sequence = jax.random.permutation(stream_key, amount)
    heavy_load, usual = shares(amount, rows * top, limit, lean, True), shares(amount, rows * top, limit, lean, False)
    places = jnp.arange(amount)

    def named(sizes, rotation):
        used = int((sizes > 0).sum())
        fixed = max(1, used // 4)
        shifted = fixed + (places - fixed + rotation * (used - fixed)) % max(1, amount - fixed)
        return jnp.zeros((amount,), jnp.int32).at[sequence[jnp.where(places < fixed, places, shifted)]].set(jnp.asarray(sizes, jnp.int32))

    sizes = jnp.where(number % 4 == 0, named(heavy_load, number // 4), named(usual, number - number // 4 - 1))
    mixed = jax.random.permutation(jax.random.fold_in(own, 3), amount)
    donor, taker = mixed[0:amount // 2 * 2:2], mixed[1:amount // 2 * 2:2]
    slack = jnp.minimum(sizes[donor] - 1, limit - sizes[taker]) // 2
    slack = jnp.where((donor == sequence[0]) | (taker == sequence[0]) | (sizes[taker] == 0), 0, jnp.maximum(slack, 0))
    shifted = jax.random.randint(jax.random.fold_in(own, 4), (amount // 2,), 0, 1 << 20) % (slack + 1)
    sizes = sizes.at[donor].add(-shifted).at[taker].add(shifted)
    members = jnp.searchsorted(jnp.cumsum(sizes), jnp.arange(rows * top), side="right").astype(jnp.int32)
    grid = members.reshape(top, rows).T
    grid = grid[jax.random.permutation(jax.random.fold_in(own, 1), rows)]
    rotation = jax.random.randint(jax.random.fold_in(own, 2), (rows, 1), 0, top)
    return jnp.take_along_axis(grid, (jnp.arange(top)[None, :] + rotation) % top, axis=1)


def shares(amount, total, most, skew, full):
    portions = [(1 << 20) // math.isqrt(grade ** skew) + 1 for grade in range(1, amount + 1)]
    largest = most if full else min(most, max(-(-total // amount), total * portions[0] // sum(portions)))
    least = 1 if total - largest >= amount - 1 else 0
    holding, spare = [largest] + [least] * (amount - 1), total - largest - least * (amount - 1)
    while spare > 0:
        free = [i for i in range(1, amount) if holding[i] < largest] or [i for i in range(1, amount) if holding[i] < most]
        mass, remaining = sum([portions[i] for i in free]), spare
        for i in free:
            addition = min(most - holding[i], max(1, remaining * portions[i] // mass), spare)
            holding[i] = holding[i] + addition
            spare = spare - addition
    return np.array(holding)


def centred(own_key, dims, scale, most, shards=(), held_as=jnp.bfloat16):
    drawn = jax.random.normal(own_key, dims, jnp.float32) * scale
    if len(shards) > 0:
        drawn = shard_levels(own_key, dims, shards, -0.22, 0.18) * drawn
    return jnp.clip(drawn, min=-most, max=most).astype(held_as)


def setup_inputs(seed: int = 0) -> dict:
    keys = jax.random.split(jax.random.key(seed), 8)
    shell_temp = centred(keys[0], (N_SPAN, ROWS, SB), 1.0, 6.0, ((0, 8), (1, 4)), jnp.float32)
    contact_gain = jnp.clip(jnp.exp(math.log(2.0) - 2.3025851 * jax.random.uniform(keys[1], (N_SPAN, ROWS, SB), jnp.float32) ** shard_levels(keys[1], (N_SPAN, ROWS, SB), ((0, 8), (1, 4)), -0.2, 0.2)), 0.2, 2.0)
    die_temp = centred(keys[2], (DZ, NX, NY), 0.5, 4.0, ((1, 8), (2, 4)), jnp.float32)
    diffusivity = jnp.clip(jnp.exp(math.log(0.12) - 1.7917595 * jax.random.uniform(keys[3], (DZ, NX, NY), jnp.float32) ** shard_levels(keys[3], (DZ, NX, NY), ((1, 8), (2, 4)), -0.2, 0.2)), 0.02, 0.12)
    routes_keys = jax.random.split(jax.random.fold_in(keys[4], 1), N_SPAN * ROWS // NB)
    routes_turns = jax.random.permutation(jax.random.fold_in(keys[4], 3), N_SPAN * ROWS // NB)
    routes = jax.vmap(lambda own, number: shared_out(jax.random.fold_in(keys[4], 2), own, number, NB, N_SPAN, 1, CAP, 2))(routes_keys, routes_turns).reshape((N_SPAN, ROWS, 1))
    tile_rows = with_ends(jax.random.randint(keys[5], (N_SPAN, ROWS), 0, CX), jax.random.fold_in(keys[5], 1), 0, CX - 1).astype(jnp.int32)
    closed = with_ends((jax.random.randint(keys[6], (N_SPAN, ROWS), 0, 4) < 3).astype(jnp.int32), jax.random.fold_in(keys[6], 1), 0, 1)
    return dict(shell_temp=shell_temp, contact_gain=contact_gain, die_temp=die_temp, diffusivity=diffusivity, routes=routes, tile_rows=tile_rows, closed=closed)


STENCIL_WEIGHT = (0.0, 1.0, 0.5, 0.25)
SHELL_RATE = 0.15
SHELL_SINK = 0.5
FACE_GAIN = 0.5


def stencil_apply(padded):
    depth_count = padded.shape[0]
    rows_inner = padded.shape[1] - 2
    cols_inner = padded.shape[2] - 2
    framed = jnp.pad(padded, ((1, 1), (0, 0), (0, 0)))
    summed = -14.0 * padded[:, 1:-1, 1:-1]
    for step_z in range(3):
        for step_x in range(3):
            for step_y in range(3):
                reach_count = abs(step_z - 1) + abs(step_x - 1) + abs(step_y - 1)
                if reach_count > 0:
                    summed = summed + STENCIL_WEIGHT[reach_count] * framed[step_z:step_z + depth_count, step_x:step_x + rows_inner, step_y:step_y + cols_inner]
    return summed


def reference(shell_temp, contact_gain, die_temp, diffusivity, routes, tile_rows, closed):
    padded = jnp.pad(shell_temp, ((0, 0), (1, 1), (1, 1)))
    laplace = padded[:, 2:, 1:-1] + padded[:, :-2, 1:-1] + padded[:, 1:-1, 2:] + padded[:, 1:-1, :-2] - 4.0 * shell_temp
    face_row = (routes[:, :, 0] * CX + tile_rows).astype(jnp.int32)
    depth_index = (jnp.arange(ROWS, dtype=jnp.int32) // NB)[None, :]
    face_grid = die_temp[0].reshape(NX, N_DEPTH, SB)
    face_values = face_grid[face_row, depth_index]
    live_mask = closed.astype(jnp.float32)[:, :, None]
    flux = contact_gain * (shell_temp - face_values) * live_mask
    shell_next = shell_temp + SHELL_RATE * laplace - SHELL_SINK * flux
    segment_ids = (face_row * N_DEPTH + depth_index).astype(jnp.int32).reshape(-1)
    heat_in = jax.ops.segment_sum(flux.reshape(-1, SB), segment_ids, num_segments=NX * N_DEPTH).reshape(NX, NY)
    field = die_temp.at[0].add(FACE_GAIN * heat_in)
    for sweep_index in range(2):
        field = field + diffusivity * stencil_apply(jnp.pad(field, ((0, 0), (1, 1), (1, 1))))
    return shell_next, field
```

```python
import functools

import jax
import jax.numpy as jnp
from jax import lax
from jax.experimental import pallas as pl
from jax.experimental.pallas import tpu as pltpu
from jax.sharding import PartitionSpec as P

SHELL_RATE = 0.15
SHELL_SINK = 0.5
FACE_GAIN = 0.5
MESH = pl.DeviceIdType.MESH
PACK = 128


def split2(x):
    hi = x.astype(jnp.bfloat16)
    lo = (x - hi.astype(jnp.float32)).astype(jnp.bfloat16)
    return hi, lo


def select_dot(select, x):
    hi, lo = split2(x)
    return jnp.dot(select, hi, preferred_element_type=jnp.float32) + jnp.dot(
        select, lo, preferred_element_type=jnp.float32
    )


def kernel(
    n, n_depth, dz, cx,
    code_ref, shell_hbm, gain_hbm, die_hbm, dif_hbm,
    shell_out, die_out,
    v0, v1, dif, shells, gain, faces, flux, partial, arrived,
    xsend, xrecv, hrows_send, hrows, colsend, cols, ucol,
    local_sem, face_send, face_recv, heat_send, heat_recv, send_sem, recv_sem,
):
    s = lax.axis_index("span")
    d = lax.axis_index("depth")
    nb = gain.shape[0]
    f32 = jnp.float32

    def exists(ds, dd):
        return (s + ds >= 0) & (s + ds < n) & (d + dd >= 0) & (d + dd < n_depth)

    def fetch(src, dst, i):
        return pltpu.make_async_copy(src, dst, local_sem.at[i])

    get_face = fetch(die_hbm.at[0], faces.at[s], 0)
    get_shell = fetch(shell_hbm, shells.at[pl.ds(8, nb)], 1)
    get_die = fetch(die_hbm, v0.at[pl.ds(1, dz), pl.ds(8, cx)], 2)
    get_gain = fetch(gain_hbm, gain, 3)
    get_dif = fetch(dif_hbm, dif, 4)
    for c in (get_face, get_shell, get_die, get_gain, get_dif):
        c.start()

    xrecv[...] = jnp.zeros_like(xrecv)
    hrows[...] = jnp.zeros_like(hrows)
    cols[...] = jnp.zeros_like(cols)
    shells[0:8, :] = jnp.zeros((8, shells.shape[1]), f32)
    shells[8 + nb : 16 + nb, :] = jnp.zeros((8, shells.shape[1]), f32)

    barrier = pltpu.get_barrier_semaphore()

    def greet(k, carry):
        pl.semaphore_signal(
            barrier, inc=1, device_id={"span": lax.rem(s + k, n), "depth": d}, device_id_type=MESH
        )
        return carry

    lax.fori_loop(1, n, greet, 0)
    count = jnp.int32(n - 1)
    for ds in (-1, 0, 1):
        for dd in (-1, 1):
            there = exists(ds, dd)
            count = count + there.astype(jnp.int32)

            @pl.when(there)
            def _():
                pl.semaphore_signal(
                    barrier, inc=1, device_id={"span": s + ds, "depth": d + dd}, device_id_type=MESH
                )

    zeros_layer = jnp.zeros(v0.shape[1:], f32)
    for buf in (v0, v1):
        buf[0] = zeros_layer
        buf[dz + 1] = zeros_layer
    pl.semaphore_wait(barrier, count)

    def face_copy(k):
        return pltpu.make_async_remote_copy(
            src_ref=faces.at[s], dst_ref=faces.at[s],
            send_sem=face_send.at[k], recv_sem=face_recv.at[k],
            device_id={"span": lax.rem(s + k, n), "depth": d}, device_id_type=MESH,
        )

    def face_arrival(k):
        return pltpu.make_async_remote_copy(
            src_ref=faces.at[s], dst_ref=faces.at[lax.rem(s + n - k, n)],
            send_sem=face_send.at[k], recv_sem=face_recv.at[k],
            device_id={"span": lax.rem(s + k, n), "depth": d}, device_id_type=MESH,
        )

    def heat_copy(k):
        to = lax.rem(s + k, n)
        return pltpu.make_async_remote_copy(
            src_ref=partial.at[to], dst_ref=arrived.at[k],
            send_sem=heat_send.at[k], recv_sem=heat_recv.at[k],
            device_id={"span": to, "depth": d}, device_id_type=MESH,
        )

    def each_partner(act):
        def step(k, carry):
            act(k)
            return carry

        lax.fori_loop(1, n, step, 0)

    get_face.wait()
    each_partner(lambda k: face_copy(k).start())

    used = [0]

    def message(src, dst, ds, dd):
        i = used[0]
        used[0] += 1
        copy = pltpu.make_async_remote_copy(
            src_ref=src, dst_ref=dst, send_sem=send_sem.at[i], recv_sem=recv_sem.at[i],
            device_id={"span": s + ds, "depth": d + dd}, device_id_type=MESH,
        )
        return copy, ds, dd

    def start(messages):
        for copy, ds, dd in messages:
            pl.when(exists(ds, dd))(copy.start)

    def wait_recv(messages):
        for copy, ds, dd in messages:
            pl.when(exists(-ds, -dd))(copy.wait_recv)

    def wait_send(messages):
        for copy, ds, dd in messages:
            pl.when(exists(ds, dd))(copy.wait_send)

    def column_messages(e):
        out = []
        for side, dd in ((0, -1), (1, 1)):
            src, dst = colsend.at[e, side], cols.at[e, 1 - side]
            out.append(message(src, dst.at[pl.ds(8, cx)], 0, dd))
            out.append(message(src.at[pl.ds(cx - 8, 8)], dst.at[pl.ds(0, 8)], 1, dd))
            out.append(message(src.at[pl.ds(0, 8)], dst.at[pl.ds(8 + cx, 8)], -1, dd))
        return out

    def row_messages(e, at, size):
        return [
            message(xsend.at[e, 0, pl.ds(at, size)], xrecv.at[e, 1, pl.ds(at, size)], -1, 0),
            message(xsend.at[e, 1, pl.ds(at, size)], xrecv.at[e, 0, pl.ds(at, size)], 1, 0),
        ]

    lane = lax.broadcasted_iota(jnp.int32, (cx, PACK), 1)

    def pack(z, layer, left, right):
        at = lane == z
        left = jnp.where(at, pltpu.roll(layer[:, :PACK], z, 1), left)
        right = jnp.where(at, pltpu.roll(layer[:, -PACK:], z + 1, 1), right)
        return left, right

    get_die.wait()

    def pack_two(i, carry):
        left, right = carry
        for j in range(2):
            z = 2 * i + j
            left, right = pack(z, v0[z + 1, 8 : 8 + cx, :], left, right)
        return left, right

    blank = jnp.zeros((cx, PACK), f32)
    left, right = lax.fori_loop(0, dz // 2, pack_two, (blank, blank))
    colsend[0, 0] = left
    colsend[0, 1] = right
    width = v0.shape[2]

    def stage_rows(e, ref):
        xsend[e, 0] = ref[1 : 1 + dz, 8, :]
        xsend[e, 1] = ref[1 : 1 + dz, 7 + cx, :]

    def place_rows(e, ref):
        ref[1 : 1 + dz, 7, :] = xrecv[e, 0]
        ref[1 : 1 + dz, 8 + cx, :] = xrecv[e, 1]

    stage_rows(0, v0)
    get_shell.wait()
    raw = row_messages(0, 0, dz) + column_messages(0)
    raw += [
        message(shells.at[pl.ds(8, 8)], shells.at[pl.ds(8 + nb, 8)], 0, -1),
        message(shells.at[pl.ds(nb, 8)], shells.at[pl.ds(0, 8)], 0, 1),
    ]
    start(raw)

    code_row = code_ref[...]
    code_col = jnp.broadcast_to(code_row, (PACK, nb)).T
    all_rows = n * cx
    step = min(256, all_rows)
    get_gain.wait()
    each_partner(lambda k: face_arrival(k).wait_recv())
    values = jnp.zeros((nb, width), f32)
    lane_rows = lax.broadcasted_iota(jnp.int32, (nb, PACK), 1).astype(f32)
    for at in range(0, all_rows, step):
        pieces = [
            jnp.where(code_col == lane_rows + float(at + j), 1.0, 0.0).astype(jnp.bfloat16)
            for j in range(0, step, PACK)
        ]
        select = jnp.concatenate(pieces, axis=1)
        part = faces[at // cx : (at + step) // cx].reshape(step, width)
        values = values + select_dot(select, part)
    live = jnp.where(code_col >= 0.0, 1.0, 0.0)
    live = jnp.concatenate([live] * (width // PACK), axis=1)
    flux[...] = gain[...] * (shells[8 : 8 + nb, :] - values) * live
    row_ids = lax.broadcasted_iota(jnp.int32, (step, nb), 0).astype(f32)
    hi, lo = split2(flux[...])
    for at in range(0, all_rows, step):
        select = jnp.where(code_row == row_ids + float(at), 1.0, 0.0).astype(jnp.bfloat16)
        heat = jnp.dot(select, hi, preferred_element_type=f32) + jnp.dot(
            select, lo, preferred_element_type=f32
        )
        partial[at // cx : (at + step) // cx] = heat.reshape(step // cx, cx, width)
    each_partner(lambda k: heat_copy(k).start())

    def filter_x(ref, z):
        return ref[z, 7 : 7 + cx, :] + ref[z, 9 : 9 + cx, :] + 2.0 * ref[z, 8 : 8 + cx, :]

    def filter_columns(c):
        p = c[7 : 7 + cx] + c[9 : 9 + cx] + 2.0 * c[8 : 8 + cx]
        return pltpu.roll(p, 1, 1) + pltpu.roll(p, PACK - 1, 1) + 2.0 * p

    def advance(ref, z, before, here, cl, cr):
        after = filter_x(ref, z + 2)
        u = before + after + 2.0 * here
        parts = [u[:, i : i + PACK] for i in range(0, width, PACK)]
        ups = [pltpu.roll(q, 1, 1) for q in parts]
        downs = [pltpu.roll(q, PACK - 1, 1) for q in parts]
        ups = [pltpu.roll(cl, lax.rem(PACK - z, PACK), 1)] + ups
        downs = downs + [pltpu.roll(cr, PACK - 1 - z, 1)]
        mixed = []
        for i, q in enumerate(parts):
            west = jnp.where(lane == 0, ups[i], ups[i + 1])
            east = jnp.where(lane == PACK - 1, downs[i + 1], downs[i])
            mixed.append(west + east + 2.0 * q)
        total = jnp.concatenate(mixed, axis=1)
        v = ref[z + 1, 8 : 8 + cx, :]
        return v + dif[z] * (0.25 * total - 16.0 * v), after

    get_dif.wait()
    wait_recv(raw)
    place_rows(0, v0)
    ucol[0] = filter_columns(cols[0, 0])
    ucol[1] = filter_columns(cols[0, 1])

    def first_two(i, carry):
        before, here, left, right = carry
        for j in range(2):
            z = 2 * i + j
            new, after = advance(v0, z, before, here, ucol[0], ucol[1])
            v1[z + 1, 8 : 8 + cx, :] = new
            left, right = pack(z, new, left, right)
            before, here = here, after
        return before, here, left, right

    _, _, left, right = lax.fori_loop(
        1, dz // 2, first_two, (filter_x(v0, 2), filter_x(v0, 3), blank, blank)
    )
    colsend[2, 0] = left
    colsend[2, 1] = right
    stage_rows(1, v1)
    late_rows = row_messages(1, 8, dz - 8)
    start(late_rows)

    each_partner(lambda k: heat_copy(k).wait_recv())

    def add_up(k, total):
        return total + arrived[k]

    heat_in = lax.fori_loop(1, n, add_up, partial[s])
    face = v0[1, 8 : 8 + cx, :] + FACE_GAIN * heat_in
    v0[1, 8 : 8 + cx, :] = face
    hrows_send[...] = face
    colsend[1, 0] = face[:, :PACK]
    colsend[1, 1] = pltpu.roll(face[:, -PACK:], 1, 1)
    heated = [
        message(hrows_send.at[pl.ds(0, 8)], hrows.at[1], -1, 0),
        message(hrows_send.at[pl.ds(cx - 8, 8)], hrows.at[0], 1, 0),
    ] + column_messages(1)
    start(heated)

    lane_s = lax.broadcasted_iota(jnp.int32, (32, width), 1)
    for r in range(0, nb, 32):
        c = shells[8 + r : 40 + r, :]
        west = jnp.where(lane_s == 0, 0.0, pltpu.roll(c, 1, 1))
        east = jnp.where(lane_s == width - 1, 0.0, pltpu.roll(c, width - 1, 1))
        lap = shells[9 + r : 41 + r, :] + shells[7 + r : 39 + r, :] + east + west - 4.0 * c
        shell_out[r : r + 32, :] = c + SHELL_RATE * lap - SHELL_SINK * flux[r : r + 32, :]

    wait_recv(heated)
    v0[1, 0:8, :] = hrows[0]
    v0[1, 8 + cx : 16 + cx, :] = hrows[1]
    lane_c = lax.broadcasted_iota(jnp.int32, (cols.shape[2], PACK), 1)
    ucol[0] = filter_columns(jnp.where(lane_c == 0, cols[1, 0], cols[0, 0]))
    ucol[1] = filter_columns(jnp.where(lane_c == 0, cols[1, 1], cols[0, 1]))
    before, here = filter_x(v0, 0), filter_x(v0, 1)
    left, right = colsend[2, 0], colsend[2, 1]
    for z in range(2):
        new, after = advance(v0, z, before, here, ucol[0], ucol[1])
        v1[z + 1, 8 : 8 + cx, :] = new
        left, right = pack(z, new, left, right)
        before, here = here, after
    colsend[2, 0] = left
    colsend[2, 1] = right
    xsend[1, 0, 0:8] = v1[1:9, 8, :]
    xsend[1, 1, 0:8] = v1[1:9, 7 + cx, :]
    last = row_messages(1, 0, 8) + column_messages(2)
    start(last)
    wait_recv(late_rows)
    wait_recv(last)
    place_rows(1, v1)
    ucol[0] = filter_columns(cols[2, 0])
    ucol[1] = filter_columns(cols[2, 1])

    def second_two(i, carry):
        before, here = carry
        for j in range(2):
            z = 2 * i + j
            new, after = advance(v1, z, before, here, ucol[0], ucol[1])
            die_out[z] = new
            before, here = here, after
        return before, here

    lax.fori_loop(0, dz // 2, second_two, (filter_x(v1, 0), filter_x(v1, 1)))

    each_partner(lambda k: face_copy(k).wait_send())
    each_partner(lambda k: heat_copy(k).wait_send())
    wait_send(raw + late_rows + heated + last)


def local(n, n_depth, shell_temp, contact_gain, die_temp, diffusivity, routes, tile_rows, closed):
    dz, cx, width = die_temp.shape
    _, nb, _ = shell_temp.shape
    code = jnp.where(closed > 0, routes[:, :, 0] * cx + tile_rows, -1).astype(jnp.float32)
    f32 = jnp.float32
    anywhere = pl.BlockSpec(memory_space=pl.ANY)
    vmem = pl.BlockSpec(memory_space=pltpu.VMEM)
    dma = pltpu.SemaphoreType.DMA
    shell_next, die_next = pl.pallas_call(
        functools.partial(kernel, n, n_depth, dz, cx),
        out_shape=(
            jax.ShapeDtypeStruct((nb, width), f32),
            jax.ShapeDtypeStruct((dz, cx, width), f32),
        ),
        in_specs=[vmem] + [anywhere] * 4,
        out_specs=(vmem, vmem),
        scratch_shapes=[
            pltpu.VMEM((dz + 2, cx + 16, width), f32),
            pltpu.VMEM((dz + 2, cx + 16, width), f32),
            pltpu.VMEM((dz, cx, width), f32),
            pltpu.VMEM((nb + 16, width), f32),
            pltpu.VMEM((nb, width), f32),
            pltpu.VMEM((n, cx, width), f32),
            pltpu.VMEM((nb, width), f32),
            pltpu.VMEM((n, cx, width), f32),
            pltpu.VMEM((n, cx, width), f32),
            pltpu.VMEM((2, 2, dz, width), f32),
            pltpu.VMEM((2, 2, dz, width), f32),
            pltpu.VMEM((cx, width), f32),
            pltpu.VMEM((2, 8, width), f32),
            pltpu.VMEM((3, 2, cx, PACK), f32),
            pltpu.VMEM((3, 2, cx + 16, PACK), f32),
            pltpu.VMEM((2, cx, PACK), f32),
            dma((5,)),
            dma((n,)),
            dma((n,)),
            dma((n,)),
            dma((n,)),
            dma((32,)),
            dma((32,)),
        ],
        compiler_params=pltpu.CompilerParams(
            collective_id=0, has_side_effects=True, vmem_limit_bytes=40 * 1024 * 1024
        ),
        cost_estimate=pl.CostEstimate(flops=20_000_000, bytes_accessed=6_000_000, transcendentals=0),
    )(code, shell_temp[0], contact_gain[0], die_temp, diffusivity)
    return shell_next[None], die_next


def solution(mesh):
    placed = (
        P("span", "depth", None),
        P("span", "depth", None),
        P(None, "span", "depth"),
        P(None, "span", "depth"),
        P("span", "depth", None),
        P("span", "depth"),
        P("span", "depth"),
    )
    return jax.shard_map(
        functools.partial(local, mesh.shape["span"], mesh.shape["depth"]),
        mesh=mesh,
        in_specs=placed,
        out_specs=(P("span", "depth", None), P(None, "span", "depth")),
        check_vma=False,
    )
```

```python
import functools

import jax
import jax.numpy as jnp
from jax import lax
from jax.experimental import pallas as pl
from jax.experimental.pallas import tpu as pltpu
from jax.sharding import PartitionSpec as P

SHELL_RATE = 0.15
SHELL_SINK = 0.5
FACE_GAIN = 0.5
MESH = pl.DeviceIdType.MESH
PACK = 128


def split2(x):
    hi = x.astype(jnp.bfloat16)
    lo = (x - hi.astype(jnp.float32)).astype(jnp.bfloat16)
    return hi, lo


def select_dot(select, x):
    hi, lo = split2(x)
    return jnp.dot(select, hi, preferred_element_type=jnp.float32) + jnp.dot(
        select, lo, preferred_element_type=jnp.float32
    )


def kernel(
    n, n_depth, dz, cx,
    shell_hbm, gain_hbm, die_hbm, dif_hbm, routes_hbm, tiles_hbm, closed_hbm,
    shell_out, die_out,
    v0, v1, dif, shells, gain, faces, flux, partial, arrived,
    xsend, xrecv, hrows_send, hrows, lrows_send, lrows, colsend, cols, ucol, codes,
    local_sem, face_send, face_recv, heat_send, heat_recv, send_sem, recv_sem,
):
    s = lax.axis_index("span")
    d = lax.axis_index("depth")
    nb = gain.shape[0]
    f32 = jnp.float32

    def exists(ds, dd):
        return (s + ds >= 0) & (s + ds < n) & (d + dd >= 0) & (d + dd < n_depth)

    def fetch(src, dst, i):
        return pltpu.make_async_copy(src, dst, local_sem.at[i])

    get_face = fetch(die_hbm.at[0], faces.at[s], 0)
    get_shell = fetch(shell_hbm, shells.at[pl.ds(8, nb)], 1)
    get_die = fetch(die_hbm, v0.at[pl.ds(1, dz), pl.ds(8, cx)], 2)
    get_gain = fetch(gain_hbm, gain, 3)
    get_dif = fetch(dif_hbm, dif, 4)
    get_codes = [
        fetch(ref, codes.at[i], 5 + i) for i, ref in enumerate((routes_hbm, tiles_hbm, closed_hbm))
    ]
    for c in [get_face, get_die, get_shell] + get_codes + [get_gain, get_dif]:
        c.start()

    xrecv[...] = jnp.zeros_like(xrecv)
    hrows[...] = jnp.zeros_like(hrows)
    lrows[...] = jnp.zeros_like(lrows)
    cols[...] = jnp.zeros_like(cols)
    shells[0:8, :] = jnp.zeros((8, shells.shape[1]), f32)
    shells[8 + nb : 16 + nb, :] = jnp.zeros((8, shells.shape[1]), f32)

    barrier = pltpu.get_barrier_semaphore()

    def greet(k, carry):
        pl.semaphore_signal(
            barrier, inc=1, device_id={"span": lax.rem(s + k, n), "depth": d}, device_id_type=MESH
        )
        return carry

    lax.fori_loop(1, n, greet, 0)
    count = jnp.int32(n - 1)
    for ds in (-1, 0, 1):
        for dd in (-1, 1):
            there = exists(ds, dd)
            count = count + there.astype(jnp.int32)

            @pl.when(there)
            def _():
                pl.semaphore_signal(
                    barrier, inc=1, device_id={"span": s + ds, "depth": d + dd}, device_id_type=MESH
                )

    zeros_layer = jnp.zeros(v0.shape[1:], f32)
    for buf in (v0, v1):
        buf[0] = zeros_layer
        buf[dz + 1] = zeros_layer
    v1[1] = zeros_layer
    v1[2] = zeros_layer
    pl.semaphore_wait(barrier, count)

    def face_copy(k):
        return pltpu.make_async_remote_copy(
            src_ref=faces.at[s], dst_ref=faces.at[s],
            send_sem=face_send.at[k], recv_sem=face_recv.at[k],
            device_id={"span": lax.rem(s + k, n), "depth": d}, device_id_type=MESH,
        )

    def face_arrival(k):
        return pltpu.make_async_remote_copy(
            src_ref=faces.at[s], dst_ref=faces.at[lax.rem(s + n - k, n)],
            send_sem=face_send.at[k], recv_sem=face_recv.at[k],
            device_id={"span": lax.rem(s + k, n), "depth": d}, device_id_type=MESH,
        )

    def heat_copy(k):
        to = lax.rem(s + k, n)
        return pltpu.make_async_remote_copy(
            src_ref=partial.at[to], dst_ref=arrived.at[k],
            send_sem=heat_send.at[k], recv_sem=heat_recv.at[k],
            device_id={"span": to, "depth": d}, device_id_type=MESH,
        )

    def each_partner(act):
        def step(k, carry):
            act(k)
            return carry

        lax.fori_loop(1, n, step, 0)

    get_face.wait()
    each_partner(lambda k: face_copy(k).start())

    used = [0]

    def message(src, dst, ds, dd):
        i = used[0]
        used[0] += 1
        copy = pltpu.make_async_remote_copy(
            src_ref=src, dst_ref=dst, send_sem=send_sem.at[i], recv_sem=recv_sem.at[i],
            device_id={"span": s + ds, "depth": d + dd}, device_id_type=MESH,
        )
        return copy, ds, dd

    def start(messages):
        for copy, ds, dd in messages:
            pl.when(exists(ds, dd))(copy.start)

    def wait_recv(messages):
        for copy, ds, dd in messages:
            pl.when(exists(-ds, -dd))(copy.wait_recv)

    def wait_send(messages):
        for copy, ds, dd in messages:
            pl.when(exists(ds, dd))(copy.wait_send)

    def column_messages(e):
        out = []
        for side, dd in ((0, -1), (1, 1)):
            src, dst = colsend.at[e, side], cols.at[e, 1 - side]
            out.append(message(src, dst.at[pl.ds(8, cx)], 0, dd))
            out.append(message(src.at[pl.ds(cx - 8, 8)], dst.at[pl.ds(0, 8)], 1, dd))
            out.append(message(src.at[pl.ds(0, 8)], dst.at[pl.ds(8 + cx, 8)], -1, dd))
        return out

    def row_messages(e):
        return [
            message(xsend.at[e, 0], xrecv.at[e, 1], -1, 0),
            message(xsend.at[e, 1], xrecv.at[e, 0], 1, 0),
        ]

    lane = lax.broadcasted_iota(jnp.int32, (cx, PACK), 1)

    def pack(z, layer, left, right):
        at = lane == z
        left = jnp.where(at, pltpu.roll(layer[:, :PACK], z, 1), left)
        right = jnp.where(at, pltpu.roll(layer[:, -PACK:], z + 1, 1), right)
        return left, right

    get_die.wait()

    def pack_some(i, carry):
        left, right = carry
        for j in range(4):
            z = 4 * i + j
            left, right = pack(z, v0[z + 1, 8 : 8 + cx, :], left, right)
        return left, right

    blank = jnp.zeros((cx, PACK), f32)
    left, right = lax.fori_loop(0, dz // 4, pack_some, (blank, blank))
    colsend[0, 0] = left
    colsend[0, 1] = right
    width = v0.shape[2]

    def stage_rows(e, ref):
        xsend[e, 0] = ref[1 : 1 + dz, 8, :]
        xsend[e, 1] = ref[1 : 1 + dz, 7 + cx, :]

    def place_rows(e, ref):
        ref[1 : 1 + dz, 7, :] = xrecv[e, 0]
        ref[1 : 1 + dz, 8 + cx, :] = xrecv[e, 1]

    stage_rows(0, v0)
    get_shell.wait()
    raw = row_messages(0) + column_messages(0)
    raw += [
        message(shells.at[pl.ds(8, 8)], shells.at[pl.ds(8 + nb, 8)], 0, -1),
        message(shells.at[pl.ds(nb, 8)], shells.at[pl.ds(0, 8)], 0, 1),
    ]
    start(raw)

    for c in get_codes:
        c.wait()
    code_row = jnp.where(codes[2] > 0, codes[0] * cx + codes[1], -1).astype(f32)
    code_col = jnp.broadcast_to(code_row, (PACK, nb)).T
    all_rows = n * cx
    step = min(256, all_rows)
    get_gain.wait()
    each_partner(lambda k: face_arrival(k).wait_recv())
    values = jnp.zeros((nb, width), f32)
    lane_rows = lax.broadcasted_iota(jnp.int32, (nb, PACK), 1).astype(f32)
    for at in range(0, all_rows, step):
        pieces = [
            jnp.where(code_col == lane_rows + float(at + j), 1.0, 0.0).astype(jnp.bfloat16)
            for j in range(0, step, PACK)
        ]
        select = jnp.concatenate(pieces, axis=1)
        part = faces[at // cx : (at + step) // cx].reshape(step, width)
        values = values + select_dot(select, part)
    live = jnp.where(code_col >= 0.0, 1.0, 0.0)
    live = jnp.concatenate([live] * (width // PACK), axis=1)
    flux[...] = gain[...] * (shells[8 : 8 + nb, :] - values) * live
    row_ids = lax.broadcasted_iota(jnp.int32, (step, nb), 0).astype(f32)
    hi, lo = split2(flux[...])
    for at in range(0, all_rows, step):
        select = jnp.where(code_row == row_ids + float(at), 1.0, 0.0).astype(jnp.bfloat16)
        heat = jnp.dot(select, hi, preferred_element_type=f32) + jnp.dot(
            select, lo, preferred_element_type=f32
        )
        partial[at // cx : (at + step) // cx] = heat.reshape(step // cx, cx, width)
    each_partner(lambda k: heat_copy(k).start())

    def filter_x(ref, z):
        return ref[z, 7 : 7 + cx, :] + ref[z, 9 : 9 + cx, :] + 2.0 * ref[z, 8 : 8 + cx, :]

    def filter_columns(c):
        p = c[7 : 7 + cx] + c[9 : 9 + cx] + 2.0 * c[8 : 8 + cx]
        return pltpu.roll(p, 1, 1) + pltpu.roll(p, PACK - 1, 1) + 2.0 * p

    def advance(ref, z, before, here, cl, cr):
        after = filter_x(ref, z + 2)
        u = before + after + 2.0 * here
        parts = [u[:, i : i + PACK] for i in range(0, width, PACK)]
        ups = [pltpu.roll(q, 1, 1) for q in parts]
        downs = [pltpu.roll(q, PACK - 1, 1) for q in parts]
        ups = [pltpu.roll(cl, lax.rem(PACK - z, PACK), 1)] + ups
        downs = downs + [pltpu.roll(cr, PACK - 1 - z, 1)]
        mixed = []
        for i, q in enumerate(parts):
            west = jnp.where(lane == 0, ups[i], ups[i + 1])
            east = jnp.where(lane == PACK - 1, downs[i + 1], downs[i])
            mixed.append(west + east + 2.0 * q)
        total = jnp.concatenate(mixed, axis=1)
        v = ref[z + 1, 8 : 8 + cx, :]
        return v + dif[z] * (0.25 * total - 16.0 * v), after

    get_dif.wait()
    wait_recv(raw)
    place_rows(0, v0)
    ucol[0] = filter_columns(cols[0, 0])
    ucol[1] = filter_columns(cols[0, 1])

    def first_two(i, carry):
        before, here, left, right = carry
        for j in range(2):
            z = 2 * i + j
            new, after = advance(v0, z, before, here, ucol[0], ucol[1])
            v1[z + 1, 8 : 8 + cx, :] = new
            left, right = pack(z, new, left, right)
            before, here = here, after
        return before, here, left, right

    _, _, left, right = lax.fori_loop(
        1, dz // 2, first_two, (filter_x(v0, 2), filter_x(v0, 3), blank, blank)
    )
    colsend[2, 0] = left
    colsend[2, 1] = right
    stage_rows(1, v1)
    early = row_messages(1) + column_messages(2)
    start(early)

    each_partner(lambda k: heat_copy(k).wait_recv())

    def add_up(k, total):
        return total + arrived[k]

    heat_in = lax.fori_loop(1, n, add_up, partial[s])
    face = v0[1, 8 : 8 + cx, :] + FACE_GAIN * heat_in
    v0[1, 8 : 8 + cx, :] = face
    hrows_send[...] = face
    colsend[1, 0] = face[:, :PACK]
    colsend[1, 1] = pltpu.roll(face[:, -PACK:], 1, 1)
    heated = [
        message(hrows_send.at[pl.ds(0, 8)], hrows.at[1], -1, 0),
        message(hrows_send.at[pl.ds(cx - 8, 8)], hrows.at[0], 1, 0),
    ] + column_messages(1)
    start(heated)

    lane_s = lax.broadcasted_iota(jnp.int32, (32, width), 1)
    for r in range(0, nb, 32):
        c = shells[8 + r : 40 + r, :]
        west = jnp.where(lane_s == 0, 0.0, pltpu.roll(c, 1, 1))
        east = jnp.where(lane_s == width - 1, 0.0, pltpu.roll(c, width - 1, 1))
        lap = shells[9 + r : 41 + r, :] + shells[7 + r : 39 + r, :] + east + west - 4.0 * c
        shell_out[r : r + 32, :] = c + SHELL_RATE * lap - SHELL_SINK * flux[r : r + 32, :]

    wait_recv(early)
    place_rows(1, v1)
    ucol[2] = filter_columns(cols[2, 0])
    ucol[3] = filter_columns(cols[2, 1])

    def second_three(i, carry):
        before, here = carry
        for j in range(3):
            z = 3 * i + j
            new, after = advance(v1, z, before, here, ucol[2], ucol[3])
            die_out[z] = new
            before, here = here, after
        return before, here

    middle = dz // 6
    state = lax.fori_loop(1, middle, second_three, (filter_x(v1, 3), filter_x(v1, 4)))

    wait_recv(heated)
    v0[1, 0:8, :] = hrows[0]
    v0[1, 8 + cx : 16 + cx, :] = hrows[1]
    lane_c = lax.broadcasted_iota(jnp.int32, (cols.shape[2], PACK), 1)
    ucol[0] = filter_columns(jnp.where(lane_c == 0, cols[1, 0], cols[0, 0]))
    ucol[1] = filter_columns(jnp.where(lane_c == 0, cols[1, 1], cols[0, 1]))
    before, here = filter_x(v0, 0), filter_x(v0, 1)
    left, right = blank, blank
    for z in range(2):
        new, after = advance(v0, z, before, here, ucol[0], ucol[1])
        v1[z + 1, 8 : 8 + cx, :] = new
        lrows_send[0, z : z + 1, :] = new[0:1]
        lrows_send[1, z : z + 1, :] = new[cx - 1 : cx]
        left, right = pack(z, new, left, right)
        before, here = here, after
    colsend[3, 0] = left
    colsend[3, 1] = right
    last = [
        message(lrows_send.at[0], lrows.at[1], -1, 0),
        message(lrows_send.at[1], lrows.at[0], 1, 0),
    ] + column_messages(3)
    start(last)

    lax.fori_loop(middle, dz // 3, second_three, state)

    wait_recv(last)
    for z in range(2):
        v1[z + 1, 7:8, :] = lrows[0, z : z + 1, :]
        v1[z + 1, 8 + cx : 9 + cx, :] = lrows[1, z : z + 1, :]
    ucol[0] = filter_columns(jnp.where(lane_c < 2, cols[3, 0], cols[2, 0]))
    ucol[1] = filter_columns(jnp.where(lane_c < 2, cols[3, 1], cols[2, 1]))
    before, here = filter_x(v1, 0), filter_x(v1, 1)
    for z in range(3):
        new, after = advance(v1, z, before, here, ucol[0], ucol[1])
        die_out[z] = new
        before, here = here, after

    each_partner(lambda k: face_copy(k).wait_send())
    each_partner(lambda k: heat_copy(k).wait_send())
    wait_send(raw + early + heated + last)


def local(n, n_depth, shell_temp, contact_gain, die_temp, diffusivity, routes, tile_rows, closed):
    dz, cx, width = die_temp.shape
    _, nb, _ = shell_temp.shape
    f32 = jnp.float32
    hbm = pl.BlockSpec(memory_space=pltpu.HBM)
    vmem = pl.BlockSpec(memory_space=pltpu.VMEM)
    dma = pltpu.SemaphoreType.DMA
    shell_next, die_next = pl.pallas_call(
        functools.partial(kernel, n, n_depth, dz, cx),
        out_shape=(
            jax.ShapeDtypeStruct((nb, width), f32),
            jax.ShapeDtypeStruct((dz, cx, width), f32),
        ),
        in_specs=[hbm] * 7,
        out_specs=(vmem, vmem),
        scratch_shapes=[
            pltpu.VMEM((dz + 2, cx + 16, width), f32),
            pltpu.VMEM((dz + 2, cx + 16, width), f32),
            pltpu.VMEM((dz, cx, width), f32),
            pltpu.VMEM((nb + 16, width), f32),
            pltpu.VMEM((nb, width), f32),
            pltpu.VMEM((n, cx, width), f32),
            pltpu.VMEM((nb, width), f32),
            pltpu.VMEM((n, cx, width), f32),
            pltpu.VMEM((n, cx, width), f32),
            pltpu.VMEM((2, 2, dz, width), f32),
            pltpu.VMEM((2, 2, dz, width), f32),
            pltpu.VMEM((cx, width), f32),
            pltpu.VMEM((2, 8, width), f32),
            pltpu.VMEM((2, 8, width), f32),
            pltpu.VMEM((2, 8, width), f32),
            pltpu.VMEM((4, 2, cx, PACK), f32),
            pltpu.VMEM((4, 2, cx + 16, PACK), f32),
            pltpu.VMEM((4, cx, PACK), f32),
            pltpu.VMEM((3, 1, nb), jnp.int32),
            dma((8,)),
            dma((n,)),
            dma((n,)),
            dma((n,)),
            dma((n,)),
            dma((40,)),
            dma((40,)),
        ],
        compiler_params=pltpu.CompilerParams(
            collective_id=0, has_side_effects=True, vmem_limit_bytes=40 * 1024 * 1024
        ),
        cost_estimate=pl.CostEstimate(flops=20_000_000, bytes_accessed=6_000_000, transcendentals=0),
    )(
        *(
            pltpu.with_memory_space_constraint(x, pltpu.HBM)
            for x in (
                shell_temp[0], contact_gain[0], die_temp, diffusivity,
                routes[:, :, 0], tile_rows, closed,
            )
        )
    )
    return shell_next[None], die_next


def solution(mesh):
    placed = (
        P("span", "depth", None),
        P("span", "depth", None),
        P(None, "span", "depth"),
        P(None, "span", "depth"),
        P("span", "depth", None),
        P("span", "depth"),
        P("span", "depth"),
    )
    return jax.shard_map(
        functools.partial(local, mesh.shape["span"], mesh.shape["depth"]),
        mesh=mesh,
        in_specs=placed,
        out_specs=(P("span", "depth", None), P(None, "span", "depth")),
        check_vma=False,
    )
```

```python
import functools

import jax
import jax.numpy as jnp
from jax import lax
from jax.experimental import pallas as pl
from jax.experimental.pallas import tpu as pltpu
from jax.sharding import PartitionSpec as P

SHELL_RATE = 0.15
SHELL_SINK = 0.5
FACE_GAIN = 0.5
MESH = pl.DeviceIdType.MESH
PACK = 128


def split2(x):
    hi = x.astype(jnp.bfloat16)
    lo = (x - hi.astype(jnp.float32)).astype(jnp.bfloat16)
    return hi, lo


def select_dot(select, x):
    hi, lo = split2(x)
    return jnp.dot(select, hi, preferred_element_type=jnp.float32) + jnp.dot(
        select, lo, preferred_element_type=jnp.float32
    )


def kernel(
    n, n_depth, dz, cx,
    shell_hbm, gain_hbm, die_hbm, dif_hbm, routes_hbm, tiles_hbm, closed_hbm,
    shell_out, die_out,
    v0, v1, dif, shells, gain, faces, flux, partial, arrived,
    xsend, xrecv, hrows_send, hrows, lrows_send, lrows, colsend, cols, ucol, codes, pick, put,
    local_sem, face_send, face_recv, heat_send, heat_recv, send_sem, recv_sem,
):
    s = lax.axis_index("span")
    d = lax.axis_index("depth")
    nb = gain.shape[0]
    f32 = jnp.float32

    def exists(ds, dd):
        return (s + ds >= 0) & (s + ds < n) & (d + dd >= 0) & (d + dd < n_depth)

    def fetch(src, dst, i):
        return pltpu.make_async_copy(src, dst, local_sem.at[i])

    get_face = fetch(die_hbm.at[0], faces.at[s], 0)
    get_shell = fetch(shell_hbm, shells.at[pl.ds(8, nb)], 1)
    get_die = fetch(die_hbm, v0.at[pl.ds(1, dz), pl.ds(8, cx)], 2)
    get_gain = fetch(gain_hbm, gain, 3)
    get_dif = fetch(dif_hbm, dif, 4)
    get_codes = [
        fetch(ref, codes.at[i], 5 + i) for i, ref in enumerate((routes_hbm, tiles_hbm, closed_hbm))
    ]
    for c in [get_face, get_die, get_shell] + get_codes + [get_gain, get_dif]:
        c.start()

    xrecv[...] = jnp.zeros_like(xrecv)
    hrows[...] = jnp.zeros_like(hrows)
    lrows[...] = jnp.zeros_like(lrows)
    cols[...] = jnp.zeros_like(cols)
    shells[0:8, :] = jnp.zeros((8, shells.shape[1]), f32)
    shells[8 + nb : 16 + nb, :] = jnp.zeros((8, shells.shape[1]), f32)

    barrier = pltpu.get_barrier_semaphore()

    def greet(k, carry):
        pl.semaphore_signal(
            barrier, inc=1, device_id={"span": lax.rem(s + k, n), "depth": d}, device_id_type=MESH
        )
        return carry

    lax.fori_loop(1, n, greet, 0)
    count = jnp.int32(n - 1)
    for ds in (-1, 0, 1):
        for dd in (-1, 1):
            there = exists(ds, dd)
            count = count + there.astype(jnp.int32)

            @pl.when(there)
            def _():
                pl.semaphore_signal(
                    barrier, inc=1, device_id={"span": s + ds, "depth": d + dd}, device_id_type=MESH
                )

    zeros_layer = jnp.zeros(v0.shape[1:], f32)
    for buf in (v0, v1):
        buf[0] = zeros_layer
        buf[dz + 1] = zeros_layer
    v1[1] = zeros_layer
    v1[2] = zeros_layer
    pl.semaphore_wait(barrier, count)

    def face_copy(k):
        return pltpu.make_async_remote_copy(
            src_ref=faces.at[s], dst_ref=faces.at[s],
            send_sem=face_send.at[k], recv_sem=face_recv.at[k],
            device_id={"span": lax.rem(s + k, n), "depth": d}, device_id_type=MESH,
        )

    def face_arrival(k):
        return pltpu.make_async_remote_copy(
            src_ref=faces.at[s], dst_ref=faces.at[lax.rem(s + n - k, n)],
            send_sem=face_send.at[k], recv_sem=face_recv.at[k],
            device_id={"span": lax.rem(s + k, n), "depth": d}, device_id_type=MESH,
        )

    def heat_copy(k):
        to = lax.rem(s + k, n)
        return pltpu.make_async_remote_copy(
            src_ref=partial.at[to], dst_ref=arrived.at[k],
            send_sem=heat_send.at[k], recv_sem=heat_recv.at[k],
            device_id={"span": to, "depth": d}, device_id_type=MESH,
        )

    def each_partner(act):
        def step(k, carry):
            act(k)
            return carry

        lax.fori_loop(1, n, step, 0)

    get_face.wait()
    each_partner(lambda k: face_copy(k).start())

    used = [0]

    def message(src, dst, ds, dd):
        i = used[0]
        used[0] += 1
        copy = pltpu.make_async_remote_copy(
            src_ref=src, dst_ref=dst, send_sem=send_sem.at[i], recv_sem=recv_sem.at[i],
            device_id={"span": s + ds, "depth": d + dd}, device_id_type=MESH,
        )
        return copy, ds, dd

    def start(messages):
        for copy, ds, dd in messages:
            pl.when(exists(ds, dd))(copy.start)

    def wait_recv(messages):
        for copy, ds, dd in messages:
            pl.when(exists(-ds, -dd))(copy.wait_recv)

    def wait_send(messages):
        for copy, ds, dd in messages:
            pl.when(exists(ds, dd))(copy.wait_send)

    def column_messages(e):
        out = []
        for side, dd in ((0, -1), (1, 1)):
            src, dst = colsend.at[e, side], cols.at[e, 1 - side]
            out.append(message(src, dst.at[pl.ds(8, cx)], 0, dd))
            out.append(message(src.at[pl.ds(cx - 8, 8)], dst.at[pl.ds(0, 8)], 1, dd))
            out.append(message(src.at[pl.ds(0, 8)], dst.at[pl.ds(8 + cx, 8)], -1, dd))
        return out

    def row_messages(e):
        return [
            message(xsend.at[e, 0], xrecv.at[e, 1], -1, 0),
            message(xsend.at[e, 1], xrecv.at[e, 0], 1, 0),
        ]

    lane = lax.broadcasted_iota(jnp.int32, (cx, PACK), 1)

    def pack(z, layer, left, right):
        at = lane == z
        left = jnp.where(at, pltpu.roll(layer[:, :PACK], z, 1), left)
        right = jnp.where(at, pltpu.roll(layer[:, -PACK:], z + 1, 1), right)
        return left, right

    get_die.wait()

    def pack_some(i, carry):
        left, right = carry
        for j in range(4):
            z = 4 * i + j
            left, right = pack(z, v0[z + 1, 8 : 8 + cx, :], left, right)
        return left, right

    blank = jnp.zeros((cx, PACK), f32)
    left, right = lax.fori_loop(0, dz // 4, pack_some, (blank, blank))
    colsend[0, 0] = left
    colsend[0, 1] = right
    width = v0.shape[2]

    def stage_rows(e, ref):
        xsend[e, 0] = ref[1 : 1 + dz, 8, :]
        xsend[e, 1] = ref[1 : 1 + dz, 7 + cx, :]

    def place_rows(e, ref):
        ref[1 : 1 + dz, 7, :] = xrecv[e, 0]
        ref[1 : 1 + dz, 8 + cx, :] = xrecv[e, 1]

    stage_rows(0, v0)
    get_shell.wait()
    raw = row_messages(0) + column_messages(0)
    raw += [
        message(shells.at[pl.ds(8, 8)], shells.at[pl.ds(8 + nb, 8)], 0, -1),
        message(shells.at[pl.ds(nb, 8)], shells.at[pl.ds(0, 8)], 0, 1),
    ]
    start(raw)

    for c in get_codes:
        c.wait()
    code_row = jnp.where(codes[2] > 0, codes[0] * cx + codes[1], -1).astype(f32)
    code_col = jnp.broadcast_to(code_row, (PACK, nb)).T
    all_rows = n * cx
    step = min(256, all_rows)
    lane_rows = lax.broadcasted_iota(jnp.int32, (nb, PACK), 1).astype(f32)
    row_ids = lax.broadcasted_iota(jnp.int32, (step, nb), 0).astype(f32)
    for at in range(0, all_rows, step):
        for j in range(at, at + step, PACK):
            pick[:, j : j + PACK] = jnp.where(code_col == lane_rows + float(j), 1.0, 0.0).astype(
                jnp.bfloat16
            )
        put[at : at + step, :] = jnp.where(code_row == row_ids + float(at), 1.0, 0.0).astype(
            jnp.bfloat16
        )
    get_gain.wait()
    each_partner(lambda k: face_arrival(k).wait_recv())
    values = jnp.zeros((nb, width), f32)
    for at in range(0, all_rows, step):
        part = faces[at // cx : (at + step) // cx].reshape(step, width)
        values = values + select_dot(pick[:, at : at + step], part)
    live = jnp.where(code_col >= 0.0, 1.0, 0.0)
    live = jnp.concatenate([live] * (width // PACK), axis=1)
    flux[...] = gain[...] * (shells[8 : 8 + nb, :] - values) * live
    hi, lo = split2(flux[...])
    for at in range(0, all_rows, step):
        select = put[at : at + step, :]
        heat = jnp.dot(select, hi, preferred_element_type=f32) + jnp.dot(
            select, lo, preferred_element_type=f32
        )
        partial[at // cx : (at + step) // cx] = heat.reshape(step // cx, cx, width)
    each_partner(lambda k: heat_copy(k).start())

    def filter_x(ref, z):
        return ref[z, 7 : 7 + cx, :] + ref[z, 9 : 9 + cx, :] + 2.0 * ref[z, 8 : 8 + cx, :]

    def filter_columns(c):
        p = c[7 : 7 + cx] + c[9 : 9 + cx] + 2.0 * c[8 : 8 + cx]
        return pltpu.roll(p, 1, 1) + pltpu.roll(p, PACK - 1, 1) + 2.0 * p

    def advance(ref, z, before, here, cl, cr):
        after = filter_x(ref, z + 2)
        u = before + after + 2.0 * here
        parts = [u[:, i : i + PACK] for i in range(0, width, PACK)]
        ups = [pltpu.roll(q, 1, 1) for q in parts]
        downs = [pltpu.roll(q, PACK - 1, 1) for q in parts]
        ups = [pltpu.roll(cl, lax.rem(PACK - z, PACK), 1)] + ups
        downs = downs + [pltpu.roll(cr, PACK - 1 - z, 1)]
        mixed = []
        for i, q in enumerate(parts):
            west = jnp.where(lane == 0, ups[i], ups[i + 1])
            east = jnp.where(lane == PACK - 1, downs[i + 1], downs[i])
            mixed.append(west + east + 2.0 * q)
        total = jnp.concatenate(mixed, axis=1)
        v = ref[z + 1, 8 : 8 + cx, :]
        return v + dif[z] * (0.25 * total - 16.0 * v), after

    get_dif.wait()
    wait_recv(raw)
    place_rows(0, v0)
    ucol[0] = filter_columns(cols[0, 0])
    ucol[1] = filter_columns(cols[0, 1])

    def first(z, carry, count):
        before, here, left, right = carry
        for j in range(count):
            new, after = advance(v0, z + j, before, here, ucol[0], ucol[1])
            v1[z + j + 1, 8 : 8 + cx, :] = new
            left, right = pack(z + j, new, left, right)
            before, here = here, after
        return before, here, left, right

    state = first(2, (filter_x(v0, 2), filter_x(v0, 3), blank, blank), 2)
    _, _, left, right = lax.fori_loop(1, dz // 4, lambda i, c: first(4 * i, c, 4), state)
    colsend[2, 0] = left
    colsend[2, 1] = right
    stage_rows(1, v1)
    early = row_messages(1) + column_messages(2)
    start(early)

    lane_s = lax.broadcasted_iota(jnp.int32, (32, width), 1)
    for r in range(0, nb, 32):
        c = shells[8 + r : 40 + r, :]
        west = jnp.where(lane_s == 0, 0.0, pltpu.roll(c, 1, 1))
        east = jnp.where(lane_s == width - 1, 0.0, pltpu.roll(c, width - 1, 1))
        lap = shells[9 + r : 41 + r, :] + shells[7 + r : 39 + r, :] + east + west - 4.0 * c
        shell_out[r : r + 32, :] = c + SHELL_RATE * lap - SHELL_SINK * flux[r : r + 32, :]

    each_partner(lambda k: heat_copy(k).wait_recv())

    def add_up(k, total):
        return total + arrived[k]

    heat_in = lax.fori_loop(1, n, add_up, partial[s])
    face = v0[1, 8 : 8 + cx, :] + FACE_GAIN * heat_in
    v0[1, 8 : 8 + cx, :] = face
    hrows_send[...] = face
    colsend[1, 0] = face[:, :PACK]
    colsend[1, 1] = pltpu.roll(face[:, -PACK:], 1, 1)
    heated = [
        message(hrows_send.at[pl.ds(0, 8)], hrows.at[1], -1, 0),
        message(hrows_send.at[pl.ds(cx - 8, 8)], hrows.at[0], 1, 0),
    ] + column_messages(1)
    start(heated)

    wait_recv(early)
    place_rows(1, v1)
    ucol[2] = filter_columns(cols[2, 0])
    ucol[3] = filter_columns(cols[2, 1])

    def second(i, carry):
        before, here = carry
        for j in range(5):
            z = 5 * i + j + 3
            new, after = advance(v1, z, before, here, ucol[2], ucol[3])
            die_out[z] = new
            before, here = here, after
        return before, here

    turns = (dz - 3) // 5
    state = lax.fori_loop(0, turns // 2, second, (filter_x(v1, 3), filter_x(v1, 4)))

    wait_recv(heated)
    v0[1, 0:8, :] = hrows[0]
    v0[1, 8 + cx : 16 + cx, :] = hrows[1]
    lane_c = lax.broadcasted_iota(jnp.int32, (cols.shape[2], PACK), 1)
    ucol[0] = filter_columns(jnp.where(lane_c == 0, cols[1, 0], cols[0, 0]))
    ucol[1] = filter_columns(jnp.where(lane_c == 0, cols[1, 1], cols[0, 1]))
    before, here = filter_x(v0, 0), filter_x(v0, 1)
    left, right = blank, blank
    for z in range(2):
        new, after = advance(v0, z, before, here, ucol[0], ucol[1])
        v1[z + 1, 8 : 8 + cx, :] = new
        lrows_send[0, z : z + 1, :] = new[0:1]
        lrows_send[1, z : z + 1, :] = new[cx - 1 : cx]
        left, right = pack(z, new, left, right)
        before, here = here, after
    colsend[3, 0] = left
    colsend[3, 1] = right
    last = [
        message(lrows_send.at[0], lrows.at[1], -1, 0),
        message(lrows_send.at[1], lrows.at[0], 1, 0),
    ] + column_messages(3)
    start(last)

    lax.fori_loop(turns // 2, turns, second, state)

    wait_recv(last)
    for z in range(2):
        v1[z + 1, 7:8, :] = lrows[0, z : z + 1, :]
        v1[z + 1, 8 + cx : 9 + cx, :] = lrows[1, z : z + 1, :]
    ucol[0] = filter_columns(jnp.where(lane_c < 2, cols[3, 0], cols[2, 0]))
    ucol[1] = filter_columns(jnp.where(lane_c < 2, cols[3, 1], cols[2, 1]))
    before, here = filter_x(v1, 0), filter_x(v1, 1)
    for z in range(3):
        new, after = advance(v1, z, before, here, ucol[0], ucol[1])
        die_out[z] = new
        before, here = here, after

    each_partner(lambda k: face_copy(k).wait_send())
    each_partner(lambda k: heat_copy(k).wait_send())
    wait_send(raw + early + heated + last)


def store(shell_in, die_in, shell_hbm, die_hbm, sems):
    dz = die_in.shape[0]
    part = dz // 4
    copies = [pltpu.make_async_copy(shell_in, shell_hbm, sems.at[4])]
    for i in range(4):
        span = pl.ds(i * part, part)
        copies.append(pltpu.make_async_copy(die_in.at[span], die_hbm.at[span], sems.at[i]))
    for c in copies:
        c.start()
    for c in copies:
        c.wait()


def local(n, n_depth, shell_temp, contact_gain, die_temp, diffusivity, routes, tile_rows, closed):
    dz, cx, width = die_temp.shape
    _, nb, _ = shell_temp.shape
    f32 = jnp.float32
    hbm = pl.BlockSpec(memory_space=pltpu.HBM)
    vmem = pl.BlockSpec(memory_space=pltpu.VMEM)
    dma = pltpu.SemaphoreType.DMA
    shell_next, die_next = pl.pallas_call(
        functools.partial(kernel, n, n_depth, dz, cx),
        out_shape=(
            jax.ShapeDtypeStruct((nb, width), f32),
            jax.ShapeDtypeStruct((dz, cx, width), f32),
        ),
        in_specs=[hbm] * 7,
        out_specs=(vmem, vmem),
        scratch_shapes=[
            pltpu.VMEM((dz + 2, cx + 16, width), f32),
            pltpu.VMEM((dz + 2, cx + 16, width), f32),
            pltpu.VMEM((dz, cx, width), f32),
            pltpu.VMEM((nb + 16, width), f32),
            pltpu.VMEM((nb, width), f32),
            pltpu.VMEM((n, cx, width), f32),
            pltpu.VMEM((nb, width), f32),
            pltpu.VMEM((n, cx, width), f32),
            pltpu.VMEM((n, cx, width), f32),
            pltpu.VMEM((2, 2, dz, width), f32),
            pltpu.VMEM((2, 2, dz, width), f32),
            pltpu.VMEM((cx, width), f32),
            pltpu.VMEM((2, 8, width), f32),
            pltpu.VMEM((2, 8, width), f32),
            pltpu.VMEM((2, 8, width), f32),
            pltpu.VMEM((4, 2, cx, PACK), f32),
            pltpu.VMEM((4, 2, cx + 16, PACK), f32),
            pltpu.VMEM((4, cx, PACK), f32),
            pltpu.VMEM((3, 1, nb), jnp.int32),
            pltpu.VMEM((nb, n * cx), jnp.bfloat16),
            pltpu.VMEM((n * cx, nb), jnp.bfloat16),
            dma((8,)),
            dma((n,)),
            dma((n,)),
            dma((n,)),
            dma((n,)),
            dma((40,)),
            dma((40,)),
        ],
        compiler_params=pltpu.CompilerParams(
            collective_id=0, has_side_effects=True, vmem_limit_bytes=40 * 1024 * 1024
        ),
        cost_estimate=pl.CostEstimate(flops=20_000_000, bytes_accessed=6_000_000, transcendentals=0),
    )(
        *(
            pltpu.with_memory_space_constraint(x, pltpu.HBM)
            for x in (
                shell_temp[0], contact_gain[0], die_temp, diffusivity,
                routes[:, :, 0], tile_rows, closed,
            )
        )
    )
    anywhere = pl.BlockSpec(memory_space=pl.ANY)
    shell_next, die_next = pl.pallas_call(
        store,
        out_shape=(
            jax.ShapeDtypeStruct((nb, width), f32),
            jax.ShapeDtypeStruct((dz, cx, width), f32),
        ),
        in_specs=[vmem, vmem],
        out_specs=(anywhere, anywhere),
        scratch_shapes=[dma((5,))],
    )(shell_next, die_next)
    return shell_next[None], die_next


def solution(mesh):
    placed = (
        P("span", "depth", None),
        P("span", "depth", None),
        P(None, "span", "depth"),
        P(None, "span", "depth"),
        P("span", "depth", None),
        P("span", "depth"),
        P("span", "depth"),
    )
    return jax.shard_map(
        functools.partial(local, mesh.shape["span"], mesh.shape["depth"]),
        mesh=mesh,
        in_specs=placed,
        out_specs=(P("span", "depth", None), P(None, "span", "depth")),
        check_vma=False,
    )
```

```python
import functools

import jax
import jax.numpy as jnp
from jax import lax
from jax.experimental import pallas as pl
from jax.experimental.pallas import tpu as pltpu
from jax.sharding import PartitionSpec as P

SHELL_RATE = 0.15
SHELL_SINK = 0.5
FACE_GAIN = 0.5
MESH = pl.DeviceIdType.MESH
PACK = 128


def split2(x):
    hi = x.astype(jnp.bfloat16)
    lo = (x - hi.astype(jnp.float32)).astype(jnp.bfloat16)
    return hi, lo


def select_dot(select, x):
    hi, lo = split2(x)
    return jnp.dot(select, hi, preferred_element_type=jnp.float32) + jnp.dot(
        select, lo, preferred_element_type=jnp.float32
    )


def kernel(
    n, n_depth, dz, cx,
    shell_hbm, gain_hbm, die_hbm, dif_hbm, routes_hbm, tiles_hbm, closed_hbm,
    shell_out, die_out,
    v0, v1, dif, shells, gain, faces, flux, partial, arrived,
    xsend, xrecv, hrows_send, hrows, lrows_send, lrows, colsend, cols, ucol, codes, pick, put,
    local_sem, face_send, face_recv, heat_send, heat_recv, send_sem, recv_sem,
):
    s = lax.axis_index("span")
    d = lax.axis_index("depth")
    nb = gain.shape[0]
    f32 = jnp.float32

    def exists(ds, dd):
        return (s + ds >= 0) & (s + ds < n) & (d + dd >= 0) & (d + dd < n_depth)

    def fetch(src, dst, i):
        return pltpu.make_async_copy(src, dst, local_sem.at[i])

    get_face = fetch(die_hbm.at[0], faces.at[s], 0)
    get_shell = fetch(shell_hbm, shells.at[pl.ds(8, nb)], 1)
    get_die = fetch(die_hbm, v0.at[pl.ds(1, dz), pl.ds(8, cx)], 2)
    get_gain = fetch(gain_hbm, gain, 3)
    get_dif = fetch(dif_hbm, dif, 4)
    get_codes = [
        fetch(ref, codes.at[i], 5 + i) for i, ref in enumerate((routes_hbm, tiles_hbm, closed_hbm))
    ]
    for c in [get_face, get_die, get_shell] + get_codes + [get_gain, get_dif]:
        c.start()

    xrecv[...] = jnp.zeros_like(xrecv)
    hrows[...] = jnp.zeros_like(hrows)
    lrows[...] = jnp.zeros_like(lrows)
    cols[...] = jnp.zeros_like(cols)
    shells[0:8, :] = jnp.zeros((8, shells.shape[1]), f32)
    shells[8 + nb : 16 + nb, :] = jnp.zeros((8, shells.shape[1]), f32)

    barrier = pltpu.get_barrier_semaphore()

    def greet(k, carry):
        pl.semaphore_signal(
            barrier, inc=1, device_id={"span": lax.rem(s + k, n), "depth": d}, device_id_type=MESH
        )
        return carry

    lax.fori_loop(1, n, greet, 0)
    count = jnp.int32(n - 1)
    for ds in (-1, 0, 1):
        for dd in (-1, 1):
            there = exists(ds, dd)
            count = count + there.astype(jnp.int32)

            @pl.when(there)
            def _():
                pl.semaphore_signal(
                    barrier, inc=1, device_id={"span": s + ds, "depth": d + dd}, device_id_type=MESH
                )

    zeros_layer = jnp.zeros(v0.shape[1:], f32)
    for buf in (v0, v1):
        buf[0] = zeros_layer
        buf[dz + 1] = zeros_layer
    v1[1] = zeros_layer
    v1[2] = zeros_layer
    pl.semaphore_wait(barrier, count)

    def face_copy(k):
        return pltpu.make_async_remote_copy(
            src_ref=faces.at[s], dst_ref=faces.at[s],
            send_sem=face_send.at[k], recv_sem=face_recv.at[k],
            device_id={"span": lax.rem(s + k, n), "depth": d}, device_id_type=MESH,
        )

    def face_arrival(k):
        return pltpu.make_async_remote_copy(
            src_ref=faces.at[s], dst_ref=faces.at[lax.rem(s + n - k, n)],
            send_sem=face_send.at[k], recv_sem=face_recv.at[k],
            device_id={"span": lax.rem(s + k, n), "depth": d}, device_id_type=MESH,
        )

    def heat_copy(k):
        to = lax.rem(s + k, n)
        return pltpu.make_async_remote_copy(
            src_ref=partial.at[to], dst_ref=arrived.at[k],
            send_sem=heat_send.at[k], recv_sem=heat_recv.at[k],
            device_id={"span": to, "depth": d}, device_id_type=MESH,
        )

    def each_partner(act):
        def step(k, carry):
            act(k)
            return carry

        lax.fori_loop(1, n, step, 0)

    get_face.wait()
    each_partner(lambda k: face_copy(k).start())

    used = [0]

    def message(src, dst, ds, dd):
        i = used[0]
        used[0] += 1
        copy = pltpu.make_async_remote_copy(
            src_ref=src, dst_ref=dst, send_sem=send_sem.at[i], recv_sem=recv_sem.at[i],
            device_id={"span": s + ds, "depth": d + dd}, device_id_type=MESH,
        )
        return copy, ds, dd

    def start(messages):
        for copy, ds, dd in messages:
            pl.when(exists(ds, dd))(copy.start)

    def wait_recv(messages):
        for copy, ds, dd in messages:
            pl.when(exists(-ds, -dd))(copy.wait_recv)

    def wait_send(messages):
        for copy, ds, dd in messages:
            pl.when(exists(ds, dd))(copy.wait_send)

    def column_messages(e):
        out = []
        for side, dd in ((0, -1), (1, 1)):
            src, dst = colsend.at[e, side], cols.at[e, 1 - side]
            out.append(message(src, dst.at[pl.ds(8, cx)], 0, dd))
            out.append(message(src.at[pl.ds(cx - 8, 8)], dst.at[pl.ds(0, 8)], 1, dd))
            out.append(message(src.at[pl.ds(0, 8)], dst.at[pl.ds(8 + cx, 8)], -1, dd))
        return out

    def row_messages(e):
        return [
            message(xsend.at[e, 0], xrecv.at[e, 1], -1, 0),
            message(xsend.at[e, 1], xrecv.at[e, 0], 1, 0),
        ]

    lane = lax.broadcasted_iota(jnp.int32, (cx, PACK), 1)

    def pack(z, layer, left, right):
        at = lane == z
        left = jnp.where(at, pltpu.roll(layer[:, :PACK], z, 1), left)
        right = jnp.where(at, pltpu.roll(layer[:, -PACK:], z + 1, 1), right)
        return left, right

    get_die.wait()

    def pack_some(i, carry):
        left, right = carry
        for j in range(8):
            z = 8 * i + j
            left, right = pack(z, v0[z + 1, 8 : 8 + cx, :], left, right)
        return left, right

    blank = jnp.zeros((cx, PACK), f32)
    left, right = lax.fori_loop(0, dz // 8, pack_some, (blank, blank))
    colsend[0, 0] = left
    colsend[0, 1] = right
    width = v0.shape[2]

    def stage_rows(e, ref):
        xsend[e, 0] = ref[1 : 1 + dz, 8, :]
        xsend[e, 1] = ref[1 : 1 + dz, 7 + cx, :]

    def place_rows(e, ref):
        ref[1 : 1 + dz, 7, :] = xrecv[e, 0]
        ref[1 : 1 + dz, 8 + cx, :] = xrecv[e, 1]

    stage_rows(0, v0)
    get_shell.wait()
    raw = row_messages(0) + column_messages(0)
    raw += [
        message(shells.at[pl.ds(8, 8)], shells.at[pl.ds(8 + nb, 8)], 0, -1),
        message(shells.at[pl.ds(nb, 8)], shells.at[pl.ds(0, 8)], 0, 1),
    ]
    start(raw)

    for c in get_codes:
        c.wait()
    code_row = jnp.where(codes[2] > 0, codes[0] * cx + codes[1], -1).astype(f32)
    code_col = jnp.broadcast_to(code_row, (PACK, nb)).T
    all_rows = n * cx
    step = min(256, all_rows)
    lane_rows = lax.broadcasted_iota(jnp.int32, (nb, PACK), 1).astype(f32)
    row_ids = lax.broadcasted_iota(jnp.int32, (step, nb), 0).astype(f32)
    for at in range(0, all_rows, step):
        for j in range(at, at + step, PACK):
            pick[:, j : j + PACK] = jnp.where(code_col == lane_rows + float(j), 1.0, 0.0).astype(
                jnp.bfloat16
            )
        put[at : at + step, :] = jnp.where(code_row == row_ids + float(at), 1.0, 0.0).astype(
            jnp.bfloat16
        )
    get_gain.wait()
    each_partner(lambda k: face_arrival(k).wait_recv())
    values = jnp.zeros((nb, width), f32)
    for at in range(0, all_rows, step):
        part = faces[at // cx : (at + step) // cx].reshape(step, width)
        values = values + select_dot(pick[:, at : at + step], part)
    live = jnp.where(code_col >= 0.0, 1.0, 0.0)
    live = jnp.concatenate([live] * (width // PACK), axis=1)
    flux[...] = gain[...] * (shells[8 : 8 + nb, :] - values) * live
    hi, lo = split2(flux[...])
    for at in range(0, all_rows, step):
        select = put[at : at + step, :]
        heat = jnp.dot(select, hi, preferred_element_type=f32) + jnp.dot(
            select, lo, preferred_element_type=f32
        )
        partial[at // cx : (at + step) // cx] = heat.reshape(step // cx, cx, width)
    each_partner(lambda k: heat_copy(k).start())

    def filter_x(ref, z):
        return ref[z, 7 : 7 + cx, :] + ref[z, 9 : 9 + cx, :] + 2.0 * ref[z, 8 : 8 + cx, :]

    def filter_columns(c):
        p = c[7 : 7 + cx] + c[9 : 9 + cx] + 2.0 * c[8 : 8 + cx]
        return pltpu.roll(p, 1, 1) + pltpu.roll(p, PACK - 1, 1) + 2.0 * p

    def advance(ref, z, before, here, cl, cr):
        after = filter_x(ref, z + 2)
        u = before + after + 2.0 * here
        parts = [u[:, i : i + PACK] for i in range(0, width, PACK)]
        ups = [pltpu.roll(q, 1, 1) for q in parts]
        downs = [pltpu.roll(q, PACK - 1, 1) for q in parts]
        ups = [pltpu.roll(cl, lax.rem(PACK - z, PACK), 1)] + ups
        downs = downs + [pltpu.roll(cr, PACK - 1 - z, 1)]
        mixed = []
        for i, q in enumerate(parts):
            west = jnp.where(lane == 0, ups[i], ups[i + 1])
            east = jnp.where(lane == PACK - 1, downs[i + 1], downs[i])
            mixed.append(west + east + 2.0 * q)
        total = jnp.concatenate(mixed, axis=1)
        v = ref[z + 1, 8 : 8 + cx, :]
        return v + dif[z] * (0.25 * total - 16.0 * v), after

    get_dif.wait()
    wait_recv(raw)
    place_rows(0, v0)
    ucol[0] = filter_columns(cols[0, 0])
    ucol[1] = filter_columns(cols[0, 1])

    def first(z, carry, count):
        before, here, left, right = carry
        for j in range(count):
            new, after = advance(v0, z + j, before, here, ucol[0], ucol[1])
            v1[z + j + 1, 8 : 8 + cx, :] = new
            left, right = pack(z + j, new, left, right)
            before, here = here, after
        return before, here, left, right

    state = first(2, (filter_x(v0, 2), filter_x(v0, 3), blank, blank), 2)
    _, _, left, right = lax.fori_loop(0, (dz - 4) // 11, lambda i, c: first(11 * i + 4, c, 11), state)
    colsend[2, 0] = left
    colsend[2, 1] = right
    stage_rows(1, v1)
    early = row_messages(1) + column_messages(2)
    start(early)

    lane_s = lax.broadcasted_iota(jnp.int32, (32, width), 1)
    for r in range(0, nb, 32):
        c = shells[8 + r : 40 + r, :]
        west = jnp.where(lane_s == 0, 0.0, pltpu.roll(c, 1, 1))
        east = jnp.where(lane_s == width - 1, 0.0, pltpu.roll(c, width - 1, 1))
        lap = shells[9 + r : 41 + r, :] + shells[7 + r : 39 + r, :] + east + west - 4.0 * c
        shell_out[r : r + 32, :] = c + SHELL_RATE * lap - SHELL_SINK * flux[r : r + 32, :]

    each_partner(lambda k: heat_copy(k).wait_recv())

    def add_up(k, total):
        return total + arrived[k]

    heat_in = lax.fori_loop(1, n, add_up, partial[s])
    face = v0[1, 8 : 8 + cx, :] + FACE_GAIN * heat_in
    v0[1, 8 : 8 + cx, :] = face
    hrows_send[...] = face
    colsend[1, 0] = face[:, :PACK]
    colsend[1, 1] = pltpu.roll(face[:, -PACK:], 1, 1)
    heated = [
        message(hrows_send.at[pl.ds(0, 8)], hrows.at[1], -1, 0),
        message(hrows_send.at[pl.ds(cx - 8, 8)], hrows.at[0], 1, 0),
    ] + column_messages(1)
    start(heated)

    wait_recv(early)
    place_rows(1, v1)
    ucol[2] = filter_columns(cols[2, 0])
    ucol[3] = filter_columns(cols[2, 1])

    def second(i, carry):
        before, here = carry
        for j in range(9):
            z = 9 * i + j + 3
            new, after = advance(v1, z, before, here, ucol[2], ucol[3])
            die_out[z] = new
            before, here = here, after
        return before, here

    turns = (dz - 3) // 9
    state = lax.fori_loop(0, turns // 2, second, (filter_x(v1, 3), filter_x(v1, 4)))

    wait_recv(heated)
    v0[1, 0:8, :] = hrows[0]
    v0[1, 8 + cx : 16 + cx, :] = hrows[1]
    lane_c = lax.broadcasted_iota(jnp.int32, (cols.shape[2], PACK), 1)
    ucol[0] = filter_columns(jnp.where(lane_c == 0, cols[1, 0], cols[0, 0]))
    ucol[1] = filter_columns(jnp.where(lane_c == 0, cols[1, 1], cols[0, 1]))
    before, here = filter_x(v0, 0), filter_x(v0, 1)
    left, right = blank, blank
    for z in range(2):
        new, after = advance(v0, z, before, here, ucol[0], ucol[1])
        v1[z + 1, 8 : 8 + cx, :] = new
        lrows_send[0, z : z + 1, :] = new[0:1]
        lrows_send[1, z : z + 1, :] = new[cx - 1 : cx]
        left, right = pack(z, new, left, right)
        before, here = here, after
    colsend[3, 0] = left
    colsend[3, 1] = right
    last = [
        message(lrows_send.at[0], lrows.at[1], -1, 0),
        message(lrows_send.at[1], lrows.at[0], 1, 0),
    ] + column_messages(3)
    start(last)

    lax.fori_loop(turns // 2, turns, second, state)

    wait_recv(last)
    for z in range(2):
        v1[z + 1, 7:8, :] = lrows[0, z : z + 1, :]
        v1[z + 1, 8 + cx : 9 + cx, :] = lrows[1, z : z + 1, :]
    ucol[0] = filter_columns(jnp.where(lane_c < 2, cols[3, 0], cols[2, 0]))
    ucol[1] = filter_columns(jnp.where(lane_c < 2, cols[3, 1], cols[2, 1]))
    before, here = filter_x(v1, 0), filter_x(v1, 1)
    for z in range(3):
        new, after = advance(v1, z, before, here, ucol[0], ucol[1])
        die_out[z] = new
        before, here = here, after

    each_partner(lambda k: face_copy(k).wait_send())
    each_partner(lambda k: heat_copy(k).wait_send())
    wait_send(raw + early + heated + last)


def local(n, n_depth, shell_temp, contact_gain, die_temp, diffusivity, routes, tile_rows, closed):
    dz, cx, width = die_temp.shape
    _, nb, _ = shell_temp.shape
    f32 = jnp.float32
    hbm = pl.BlockSpec(memory_space=pltpu.HBM)
    vmem = pl.BlockSpec(memory_space=pltpu.VMEM)
    dma = pltpu.SemaphoreType.DMA
    shell_next, die_next = pl.pallas_call(
        functools.partial(kernel, n, n_depth, dz, cx),
        out_shape=(
            jax.ShapeDtypeStruct((nb, width), f32),
            jax.ShapeDtypeStruct((dz, cx, width), f32),
        ),
        in_specs=[hbm] * 7,
        out_specs=(vmem, vmem),
        scratch_shapes=[
            pltpu.VMEM((dz + 2, cx + 16, width), f32),
            pltpu.VMEM((dz + 2, cx + 16, width), f32),
            pltpu.VMEM((dz, cx, width), f32),
            pltpu.VMEM((nb + 16, width), f32),
            pltpu.VMEM((nb, width), f32),
            pltpu.VMEM((n, cx, width), f32),
            pltpu.VMEM((nb, width), f32),
            pltpu.VMEM((n, cx, width), f32),
            pltpu.VMEM((n, cx, width), f32),
            pltpu.VMEM((2, 2, dz, width), f32),
            pltpu.VMEM((2, 2, dz, width), f32),
            pltpu.VMEM((cx, width), f32),
            pltpu.VMEM((2, 8, width), f32),
            pltpu.VMEM((2, 8, width), f32),
            pltpu.VMEM((2, 8, width), f32),
            pltpu.VMEM((4, 2, cx, PACK), f32),
            pltpu.VMEM((4, 2, cx + 16, PACK), f32),
            pltpu.VMEM((4, cx, PACK), f32),
            pltpu.VMEM((3, 1, nb), jnp.int32),
            pltpu.VMEM((nb, n * cx), jnp.bfloat16),
            pltpu.VMEM((n * cx, nb), jnp.bfloat16),
            dma((8,)),
            dma((n,)),
            dma((n,)),
            dma((n,)),
            dma((n,)),
            dma((40,)),
            dma((40,)),
        ],
        compiler_params=pltpu.CompilerParams(
            collective_id=0, has_side_effects=True, vmem_limit_bytes=40 * 1024 * 1024
        ),
        cost_estimate=pl.CostEstimate(flops=20_000_000, bytes_accessed=6_000_000, transcendentals=0),
    )(
        *(
            pltpu.with_memory_space_constraint(x, pltpu.HBM)
            for x in (
                shell_temp[0], contact_gain[0], die_temp, diffusivity,
                routes[:, :, 0], tile_rows, closed,
            )
        )
    )
    return shell_next[None], die_next


def solution(mesh):
    placed = (
        P("span", "depth", None),
        P("span", "depth", None),
        P(None, "span", "depth"),
        P(None, "span", "depth"),
        P("span", "depth", None),
        P("span", "depth"),
        P("span", "depth"),
    )
    return jax.shard_map(
        functools.partial(local, mesh.shape["span"], mesh.shape["depth"]),
        mesh=mesh,
        in_specs=placed,
        out_specs=(P("span", "depth", None), P(None, "span", "depth")),
        check_vma=False,
    )
```

```python
import functools

import jax
import jax.numpy as jnp
from jax import lax
from jax.experimental import pallas as pl
from jax.experimental.pallas import tpu as pltpu
from jax.sharding import PartitionSpec as P

SHELL_RATE = 0.15
SHELL_SINK = 0.5
FACE_GAIN = 0.5
MESH = pl.DeviceIdType.MESH
PACK = 128


def split2(x):
    hi = x.astype(jnp.bfloat16)
    lo = (x - hi.astype(jnp.float32)).astype(jnp.bfloat16)
    return hi, lo


def select_dot(select, x):
    hi, lo = split2(x)
    return jnp.dot(select, hi, preferred_element_type=jnp.float32) + jnp.dot(
        select, lo, preferred_element_type=jnp.float32
    )


def kernel(
    n, n_depth, dz, cx,
    shell_hbm, gain_hbm, die_hbm, dif_hbm, routes_hbm, tiles_hbm, closed_hbm,
    shell_out, die_out,
    v0, v1, dif, shells, gain, faces, flux, partial, arrived,
    xsend, xrecv, hrows_send, hrows, lrows_send, lrows, colsend, cols, ucol, codes, pick, put,
    local_sem, face_send, face_recv, heat_send, heat_recv, send_sem, recv_sem,
):
    s = lax.axis_index("span")
    d = lax.axis_index("depth")
    nb = gain.shape[0]
    f32 = jnp.float32

    def exists(ds, dd):
        return (s + ds >= 0) & (s + ds < n) & (d + dd >= 0) & (d + dd < n_depth)

    def fetch(src, dst, i):
        return pltpu.make_async_copy(src, dst, local_sem.at[i])

    get_face = fetch(die_hbm.at[0], faces.at[s], 0)
    get_shell = fetch(shell_hbm, shells.at[pl.ds(8, nb)], 1)
    get_die = fetch(die_hbm, v0.at[pl.ds(1, dz), pl.ds(8, cx)], 2)
    get_gain = fetch(gain_hbm, gain, 3)
    get_dif = fetch(dif_hbm, dif, 4)
    get_codes = [
        fetch(ref, codes.at[i], 5 + i) for i, ref in enumerate((routes_hbm, tiles_hbm, closed_hbm))
    ]
    for c in [get_face, get_die, get_shell] + get_codes + [get_gain, get_dif]:
        c.start()

    xrecv[...] = jnp.zeros_like(xrecv)
    hrows[...] = jnp.zeros_like(hrows)
    lrows[...] = jnp.zeros_like(lrows)
    cols[...] = jnp.zeros_like(cols)
    shells[0:8, :] = jnp.zeros((8, shells.shape[1]), f32)
    shells[8 + nb : 16 + nb, :] = jnp.zeros((8, shells.shape[1]), f32)

    barrier = pltpu.get_barrier_semaphore()

    def greet(k, carry):
        pl.semaphore_signal(
            barrier, inc=1, device_id={"span": lax.rem(s + k, n), "depth": d}, device_id_type=MESH
        )
        return carry

    lax.fori_loop(1, n, greet, 0)
    count = jnp.int32(n - 1)
    for ds in (-1, 0, 1):
        for dd in (-1, 1):
            there = exists(ds, dd)
            count = count + there.astype(jnp.int32)

            @pl.when(there)
            def _():
                pl.semaphore_signal(
                    barrier, inc=1, device_id={"span": s + ds, "depth": d + dd}, device_id_type=MESH
                )

    zeros_layer = jnp.zeros(v0.shape[1:], f32)
    for buf in (v0, v1):
        buf[0] = zeros_layer
        buf[dz + 1] = zeros_layer
    v1[1] = zeros_layer
    v1[2] = zeros_layer
    pl.semaphore_wait(barrier, count)

    def face_copy(k):
        return pltpu.make_async_remote_copy(
            src_ref=faces.at[s], dst_ref=faces.at[s],
            send_sem=face_send.at[k], recv_sem=face_recv.at[k],
            device_id={"span": lax.rem(s + k, n), "depth": d}, device_id_type=MESH,
        )

    def face_arrival(k):
        return pltpu.make_async_remote_copy(
            src_ref=faces.at[s], dst_ref=faces.at[lax.rem(s + n - k, n)],
            send_sem=face_send.at[k], recv_sem=face_recv.at[k],
            device_id={"span": lax.rem(s + k, n), "depth": d}, device_id_type=MESH,
        )

    def heat_copy(k):
        to = lax.rem(s + k, n)
        return pltpu.make_async_remote_copy(
            src_ref=partial.at[to], dst_ref=arrived.at[k],
            send_sem=heat_send.at[k], recv_sem=heat_recv.at[k],
            device_id={"span": to, "depth": d}, device_id_type=MESH,
        )

    def each_partner(act):
        def step(k, carry):
            act(k)
            return carry

        lax.fori_loop(1, n, step, 0)

    get_face.wait()
    each_partner(lambda k: face_copy(k).start())

    used = [0]

    def message(src, dst, ds, dd):
        i = used[0]
        used[0] += 1
        copy = pltpu.make_async_remote_copy(
            src_ref=src, dst_ref=dst, send_sem=send_sem.at[i], recv_sem=recv_sem.at[i],
            device_id={"span": s + ds, "depth": d + dd}, device_id_type=MESH,
        )
        return copy, ds, dd

    def start(messages):
        for copy, ds, dd in messages:
            pl.when(exists(ds, dd))(copy.start)

    def wait_recv(messages):
        for copy, ds, dd in messages:
            pl.when(exists(-ds, -dd))(copy.wait_recv)

    def wait_send(messages):
        for copy, ds, dd in messages:
            pl.when(exists(ds, dd))(copy.wait_send)

    def column_messages(e):
        out = []
        for side, dd in ((0, -1), (1, 1)):
            src, dst = colsend.at[e, side], cols.at[e, 1 - side]
            out.append(message(src, dst.at[pl.ds(8, cx)], 0, dd))
            out.append(message(src.at[pl.ds(cx - 8, 8)], dst.at[pl.ds(0, 8)], 1, dd))
            out.append(message(src.at[pl.ds(0, 8)], dst.at[pl.ds(8 + cx, 8)], -1, dd))
        return out

    def row_messages(e):
        return [
            message(xsend.at[e, 0], xrecv.at[e, 1], -1, 0),
            message(xsend.at[e, 1], xrecv.at[e, 0], 1, 0),
        ]

    lane = lax.broadcasted_iota(jnp.int32, (cx, PACK), 1)

    def pack(z, layer, left, right):
        at = lane == z
        left = jnp.where(at, pltpu.roll(layer[:, :PACK], z, 1), left)
        right = jnp.where(at, pltpu.roll(layer[:, -PACK:], z + 1, 1), right)
        return left, right

    get_die.wait()

    def pack_some(i, carry):
        left, right = carry
        for j in range(8):
            z = 8 * i + j
            left, right = pack(z, v0[z + 1, 8 : 8 + cx, :], left, right)
        return left, right

    blank = jnp.zeros((cx, PACK), f32)
    left, right = lax.fori_loop(0, dz // 8, pack_some, (blank, blank))
    colsend[0, 0] = left
    colsend[0, 1] = right
    width = v0.shape[2]

    def stage_rows(e, ref):
        xsend[e, 0] = ref[1 : 1 + dz, 8, :]
        xsend[e, 1] = ref[1 : 1 + dz, 7 + cx, :]

    def place_rows(e, ref):
        ref[1 : 1 + dz, 7, :] = xrecv[e, 0]
        ref[1 : 1 + dz, 8 + cx, :] = xrecv[e, 1]

    stage_rows(0, v0)
    get_shell.wait()
    raw = row_messages(0) + column_messages(0)
    raw += [
        message(shells.at[pl.ds(8, 8)], shells.at[pl.ds(8 + nb, 8)], 0, -1),
        message(shells.at[pl.ds(nb, 8)], shells.at[pl.ds(0, 8)], 0, 1),
    ]
    start(raw)

    for c in get_codes:
        c.wait()
    code_row = jnp.where(codes[2] > 0, codes[0] * cx + codes[1], -1).astype(f32)
    code_col = jnp.broadcast_to(code_row, (PACK, nb)).T
    all_rows = n * cx
    step = min(256, all_rows)
    lane_rows = lax.broadcasted_iota(jnp.int32, (nb, PACK), 1).astype(f32)
    row_ids = lax.broadcasted_iota(jnp.int32, (step, nb), 0).astype(f32)
    for at in range(0, all_rows, step):
        for j in range(at, at + step, PACK):
            pick[:, j : j + PACK] = jnp.where(code_col == lane_rows + float(j), 1.0, 0.0).astype(
                jnp.bfloat16
            )
        put[at : at + step, :] = jnp.where(code_row == row_ids + float(at), 1.0, 0.0).astype(
            jnp.bfloat16
        )
    get_gain.wait()
    each_partner(lambda k: face_arrival(k).wait_recv())
    values = jnp.zeros((nb, width), f32)
    for at in range(0, all_rows, step):
        part = faces[at // cx : (at + step) // cx].reshape(step, width)
        values = values + select_dot(pick[:, at : at + step], part)
    live = jnp.where(code_col >= 0.0, 1.0, 0.0)
    live = jnp.concatenate([live] * (width // PACK), axis=1)
    flux[...] = gain[...] * (shells[8 : 8 + nb, :] - values) * live
    hi, lo = split2(flux[...])
    for at in range(0, all_rows, step):
        select = put[at : at + step, :]
        heat = jnp.dot(select, hi, preferred_element_type=f32) + jnp.dot(
            select, lo, preferred_element_type=f32
        )
        partial[at // cx : (at + step) // cx] = heat.reshape(step // cx, cx, width)
    each_partner(lambda k: heat_copy(k).start())

    def filter_x(ref, z):
        return ref[z, 7 : 7 + cx, :] + ref[z, 9 : 9 + cx, :] + 2.0 * ref[z, 8 : 8 + cx, :]

    def filter_columns(c):
        p = c[7 : 7 + cx] + c[9 : 9 + cx] + 2.0 * c[8 : 8 + cx]
        return pltpu.roll(p, 1, 1) + pltpu.roll(p, PACK - 1, 1) + 2.0 * p

    def advance(ref, z, before, here, cl, cr):
        after = filter_x(ref, z + 2)
        u = before + after + 2.0 * here
        parts = [u[:, i : i + PACK] for i in range(0, width, PACK)]
        ups = [pltpu.roll(q, 1, 1) for q in parts]
        downs = [pltpu.roll(q, PACK - 1, 1) for q in parts]
        ups = [pltpu.roll(cl, lax.rem(PACK - z, PACK), 1)] + ups
        downs = downs + [pltpu.roll(cr, PACK - 1 - z, 1)]
        mixed = []
        for i, q in enumerate(parts):
            west = jnp.where(lane == 0, ups[i], ups[i + 1])
            east = jnp.where(lane == PACK - 1, downs[i + 1], downs[i])
            mixed.append(west + east + 2.0 * q)
        total = jnp.concatenate(mixed, axis=1)
        v = ref[z + 1, 8 : 8 + cx, :]
        return v + dif[z] * (0.25 * total - 16.0 * v), after

    get_dif.wait()
    wait_recv(raw)
    place_rows(0, v0)
    ucol[0] = filter_columns(cols[0, 0])
    ucol[1] = filter_columns(cols[0, 1])

    def first(z, carry, count):
        before, here, left, right = carry
        for j in range(count):
            new, after = advance(v0, z + j, before, here, ucol[0], ucol[1])
            v1[z + j + 1, 8 : 8 + cx, :] = new
            left, right = pack(z + j, new, left, right)
            before, here = here, after
        return before, here, left, right

    state = first(2, (filter_x(v0, 2), filter_x(v0, 3), blank, blank), 2)
    _, _, left, right = lax.fori_loop(0, (dz - 4) // 11, lambda i, c: first(11 * i + 4, c, 11), state)
    colsend[2, 0] = left
    colsend[2, 1] = right
    stage_rows(1, v1)
    early = row_messages(1) + column_messages(2)
    start(early)

    each_partner(lambda k: heat_copy(k).wait_recv())

    def add_up(k, total):
        return total + arrived[k]

    heat_in = lax.fori_loop(1, n, add_up, partial[s])
    face = v0[1, 8 : 8 + cx, :] + FACE_GAIN * heat_in
    v0[1, 8 : 8 + cx, :] = face
    hrows_send[...] = face
    colsend[1, 0] = face[:, :PACK]
    colsend[1, 1] = pltpu.roll(face[:, -PACK:], 1, 1)
    heated = [
        message(hrows_send.at[pl.ds(0, 8)], hrows.at[1], -1, 0),
        message(hrows_send.at[pl.ds(cx - 8, 8)], hrows.at[0], 1, 0),
    ] + column_messages(1)
    start(heated)

    lane_s = lax.broadcasted_iota(jnp.int32, (32, width), 1)
    for r in range(0, nb, 32):
        c = shells[8 + r : 40 + r, :]
        west = jnp.where(lane_s == 0, 0.0, pltpu.roll(c, 1, 1))
        east = jnp.where(lane_s == width - 1, 0.0, pltpu.roll(c, width - 1, 1))
        lap = shells[9 + r : 41 + r, :] + shells[7 + r : 39 + r, :] + east + west - 4.0 * c
        shell_out[r : r + 32, :] = c + SHELL_RATE * lap - SHELL_SINK * flux[r : r + 32, :]

    wait_recv(early)
    place_rows(1, v1)
    ucol[2] = filter_columns(cols[2, 0])
    ucol[3] = filter_columns(cols[2, 1])

    def second(i, carry):
        before, here = carry
        for j in range(9):
            z = 9 * i + j + 3
            new, after = advance(v1, z, before, here, ucol[2], ucol[3])
            die_out[z] = new
            before, here = here, after
        return before, here

    turns = (dz - 3) // 9
    state = lax.fori_loop(0, turns // 2, second, (filter_x(v1, 3), filter_x(v1, 4)))

    wait_recv(heated)
    v0[1, 0:8, :] = hrows[0]
    v0[1, 8 + cx : 16 + cx, :] = hrows[1]
    lane_c = lax.broadcasted_iota(jnp.int32, (cols.shape[2], PACK), 1)
    ucol[0] = filter_columns(jnp.where(lane_c == 0, cols[1, 0], cols[0, 0]))
    ucol[1] = filter_columns(jnp.where(lane_c == 0, cols[1, 1], cols[0, 1]))
    before, here = filter_x(v0, 0), filter_x(v0, 1)
    left, right = blank, blank
    for z in range(2):
        new, after = advance(v0, z, before, here, ucol[0], ucol[1])
        v1[z + 1, 8 : 8 + cx, :] = new
        lrows_send[0, z : z + 1, :] = new[0:1]
        lrows_send[1, z : z + 1, :] = new[cx - 1 : cx]
        left, right = pack(z, new, left, right)
        before, here = here, after
    colsend[3, 0] = left
    colsend[3, 1] = right
    last = [
        message(lrows_send.at[0], lrows.at[1], -1, 0),
        message(lrows_send.at[1], lrows.at[0], 1, 0),
    ] + column_messages(3)
    start(last)

    lax.fori_loop(turns // 2, turns, second, state)

    wait_recv(last)
    for z in range(2):
        v1[z + 1, 7:8, :] = lrows[0, z : z + 1, :]
        v1[z + 1, 8 + cx : 9 + cx, :] = lrows[1, z : z + 1, :]
    ucol[0] = filter_columns(jnp.where(lane_c < 2, cols[3, 0], cols[2, 0]))
    ucol[1] = filter_columns(jnp.where(lane_c < 2, cols[3, 1], cols[2, 1]))
    before, here = filter_x(v1, 0), filter_x(v1, 1)
    for z in range(3):
        new, after = advance(v1, z, before, here, ucol[0], ucol[1])
        die_out[z] = new
        before, here = here, after

    each_partner(lambda k: face_copy(k).wait_send())
    each_partner(lambda k: heat_copy(k).wait_send())
    wait_send(raw + early + heated + last)


def local(n, n_depth, shell_temp, contact_gain, die_temp, diffusivity, routes, tile_rows, closed):
    dz, cx, width = die_temp.shape
    _, nb, _ = shell_temp.shape
    f32 = jnp.float32
    hbm = pl.BlockSpec(memory_space=pltpu.HBM)
    vmem = pl.BlockSpec(memory_space=pltpu.VMEM)
    dma = pltpu.SemaphoreType.DMA
    shell_next, die_next = pl.pallas_call(
        functools.partial(kernel, n, n_depth, dz, cx),
        out_shape=(
            jax.ShapeDtypeStruct((nb, width), f32),
            jax.ShapeDtypeStruct((dz, cx, width), f32),
        ),
        in_specs=[hbm] * 7,
        out_specs=(vmem, vmem),
        scratch_shapes=[
            pltpu.VMEM((dz + 2, cx + 16, width), f32),
            pltpu.VMEM((dz + 2, cx + 16, width), f32),
            pltpu.VMEM((dz, cx, width), f32),
            pltpu.VMEM((nb + 16, width), f32),
            pltpu.VMEM((nb, width), f32),
            pltpu.VMEM((n, cx, width), f32),
            pltpu.VMEM((nb, width), f32),
            pltpu.VMEM((n, cx, width), f32),
            pltpu.VMEM((n, cx, width), f32),
            pltpu.VMEM((2, 2, dz, width), f32),
            pltpu.VMEM((2, 2, dz, width), f32),
            pltpu.VMEM((cx, width), f32),
            pltpu.VMEM((2, 8, width), f32),
            pltpu.VMEM((2, 8, width), f32),
            pltpu.VMEM((2, 8, width), f32),
            pltpu.VMEM((4, 2, cx, PACK), f32),
            pltpu.VMEM((4, 2, cx + 16, PACK), f32),
            pltpu.VMEM((4, cx, PACK), f32),
            pltpu.VMEM((3, 1, nb), jnp.int32),
            pltpu.VMEM((nb, n * cx), jnp.bfloat16),
            pltpu.VMEM((n * cx, nb), jnp.bfloat16),
            dma((8,)),
            dma((n,)),
            dma((n,)),
            dma((n,)),
            dma((n,)),
            dma((40,)),
            dma((40,)),
        ],
        compiler_params=pltpu.CompilerParams(
            collective_id=0, has_side_effects=True, vmem_limit_bytes=40 * 1024 * 1024
        ),
        cost_estimate=pl.CostEstimate(flops=20_000_000, bytes_accessed=6_000_000, transcendentals=0),
    )(
        *(
            pltpu.with_memory_space_constraint(x, pltpu.HBM)
            for x in (
                shell_temp[0], contact_gain[0], die_temp, diffusivity,
                routes[:, :, 0], tile_rows, closed,
            )
        )
    )
    return shell_next[None], die_next


def solution(mesh):
    placed = (
        P("span", "depth", None),
        P("span", "depth", None),
        P(None, "span", "depth"),
        P(None, "span", "depth"),
        P("span", "depth", None),
        P("span", "depth"),
        P("span", "depth"),
    )
    return jax.shard_map(
        functools.partial(local, mesh.shape["span"], mesh.shape["depth"]),
        mesh=mesh,
        in_specs=placed,
        out_specs=(P("span", "depth", None), P(None, "span", "depth")),
        check_vma=False,
    )
```
